256 devices in a mesh: row: 4 (over x), col: 4 (over y), depth: 16 (over z, core).
Axes of the slice: x: 4, y: 4, z: 8, core: 2. Of those that a mesh axis runs over, the one named last changes fastest.
Arguments:
- activations: bfloat16 [8192, 14848], P(('row', 'depth'), 'col'), may hold values from -0.1875 to 0.1875
- pre_act: bfloat16 [8192, 8192], P(('col', 'depth'), 'row'), may hold values from -8 to 8
- grad_act: bfloat16 [8192, 8192], P(('col', 'depth'), 'row'), may hold values from -6 to 6
- quant_weight: bfloat16 [14848, 8192], P('col', 'row'), may hold values from -0.046875 to 0.046875
- block_scale: float32 [116, 8192], P('col', 'row'), may hold values from 0.5 to 2
Outputs:
- grad_input: bfloat16 [8192, 14848], P(('row', 'depth'), 'col')
- grad_weight: bfloat16 [14848, 8192], P(('col', 'depth'), 'row')
The draws below stay inside these ranges and needn't reach their ends.
All inputs are finite; a program needn't handle non-finite values.
Results may differ from the reference program's by a relative error of at most 0.0058.
Values may be sent and summed in bfloat16 or wider, within the bound.
A program may use at most 192 MiB of HBM per device.

```python
import math
import jax
import jax.numpy as jnp
from jax import lax

D = 14848
FF = 8192
BLOCK = 128
TOKENS = 8192


def spiked(array, key, source, target, parts, factor):
    owner, partner = [(jnp.arange(array.shape[axis_at]) // (array.shape[axis_at] // parts)).reshape([-1 if axis == axis_at else 1 for axis in range(array.ndim)]) for axis_at in (source, target)]
    chosen = jax.random.permutation(key, parts)[partner]
    strong = (owner == chosen) | (owner == (partner + parts // 2) % parts)
    return jnp.where(strong, factor * array, array)


def level_of(key, extent, pieces, low, high):
    def one(dim, shards_of):
        steps = jax.random.uniform(jax.random.fold_in(jax.random.fold_in(key, 6), dim), (shards_of,), jnp.float32, low / len(pieces), high / len(pieces))
        return jnp.repeat(jnp.exp(steps), extent[dim] // shards_of).reshape((-1,) + (1,) * (len(extent) - dim - 1))

    factor_of = one(*pieces[0])
    for cut in pieces[1:]:
        factor_of = factor_of * one(*cut)
    return factor_of


def scatter_about(stream_key, shape, spread, limit, pieces=(), dtype=jnp.bfloat16):
    drawn = jax.random.normal(stream_key, shape, jnp.float32) * spread
    if len(pieces) > 0:
        drawn = level_of(stream_key, shape, pieces, -0.22, 0.18) * drawn
    return jnp.clip(drawn, min=-limit, max=limit).astype(dtype)


def gaussian_with(stream_key, dims, deviation, limit, split, heavy, dtype=jnp.bfloat16):
    entries = deviation * jax.random.normal(stream_key, dims, jnp.float32)
    if split:
        entries = entries * level_of(stream_key, dims, split, -0.22, 0.18)
    return jnp.clip(spiked(entries, jax.random.fold_in(stream_key, 3), *heavy), -limit, limit).astype(dtype)


def setup_inputs(seed: int = 0) -> dict:
    seeds = jax.random.split(jax.random.key(seed), 6)
    return {
        "activations": gaussian_with(seeds[0], (TOKENS, D), (TOKENS ** -0.5), 0.1875, ((0, 64), (1, 4)), (0, 1, 64, 4.0)),
        "pre_act": scatter_about(seeds[1], (TOKENS, FF), 1.5, 8.0, ((0, 64), (1, 4))),
        "grad_act": scatter_about(seeds[2], (TOKENS, FF), 1.0, 6.0, ((0, 64), (1, 4))),
        "quant_weight": scatter_about(seeds[3], (D, FF), D ** -0.5, 0.046875, ((0, 4), (1, 4))),
        "block_scale": jnp.clip(jnp.exp(math.log(2.0) - 1.3862944 * jax.random.uniform(seeds[4], (D // BLOCK, FF), jnp.float32) ** level_of(seeds[4], (D // BLOCK, FF), ((0, 4), (1, 4)), -0.2, 0.2)), 0.5, 2.0),
    }


inv_sqrt_two = 0.7071067811865476
inv_sqrt_tau = 0.3989422804014327

def gelu_slope(values):
    return 0.5 * (1.0 + lax.erf(values * inv_sqrt_two)) + values * jnp.exp(-0.5 * values * values) * inv_sqrt_tau

def reference(activations, pre_act, grad_act, quant_weight, block_scale):
    scaled = quant_weight.astype(jnp.float32).reshape(D // BLOCK, BLOCK, FF) * block_scale[:, None, :]
    weight = scaled.reshape(D, FF).astype(jnp.bfloat16)
    grad_pre = (grad_act.astype(jnp.float32) * gelu_slope(pre_act.astype(jnp.float32))).astype(jnp.bfloat16)
    grad_input = jnp.dot(grad_pre, weight.T, preferred_element_type=jnp.float32).astype(jnp.bfloat16)
    grad_weight = jnp.dot(activations.T, grad_pre, preferred_element_type=jnp.float32).astype(jnp.bfloat16)
    return (grad_input, grad_weight)
```

```python
import jax
import jax.numpy as jnp
from jax import lax
from jax.experimental import pallas as pl
from jax.experimental.pallas import tpu as pltpu
from jax.sharding import PartitionSpec as P

MESH = pl.DeviceIdType.MESH
BF16, F32 = jnp.bfloat16, jnp.float32
NX, NY, NZ = 4, 4, 8
TOK = 128
FL = 2048
DL = 3712
CH = 232
FQ = 512
PAIR = 256
NP = 7
BASE = 1920
MID = 1792

inv_sqrt_two = 0.7071067811865476
inv_sqrt_tau = 0.3989422804014327


def gelu_slope(values):
    return (
        0.5 * (1.0 + lax.erf(values * inv_sqrt_two))
        + values * jnp.exp(-0.5 * values * values) * inv_sqrt_tau
    )


def kernel(
    acts_h, pre_h, grad_h, qw_h, scale_h, gi_h, gw_h,
    acts, pre, grad, scale, wq, wm, at32, asend, at, gb, zs, zr,
    gis, gism, gir, girm, gsx, go, gwo,
    in_sem, w_sem, a_send, a_recv, g_send, g_recv, f_send, f_recv,
    z_send, z_recv, i_send, i_recv, s_send, s_recv, out_sem,
):
    x, y, depth = lax.axis_index("row"), lax.axis_index("col"), lax.axis_index("depth")
    z, c = depth // 2, lax.rem(depth, 2)
    oc = 1 - c

    def dev(dx, dy, dz, core):
        return (
            lax.rem(x + dx, NX),
            lax.rem(y + dy, NY),
            lax.rem(z + dz, NZ) * 2 + core,
        )

    def remote(src, dst, send, recv, where):
        pltpu.make_async_remote_copy(
            src_ref=src, dst_ref=dst, send_sem=send, recv_sem=recv,
            device_id=where, device_id_type=MESH,
        ).start()

    def wait(ref, sem):
        pltpu.make_async_copy(ref, ref, sem).wait()

    loads = [
        pltpu.make_async_copy(pre_h, pre, in_sem.at[0]),
        pltpu.make_async_copy(grad_h, grad, in_sem.at[1]),
        pltpu.make_async_copy(acts_h, acts, in_sem.at[2]),
        pltpu.make_async_copy(scale_h, scale, in_sem.at[3]),
    ]
    for cp in loads:
        cp.start()
    w_loads = [
        pltpu.make_async_copy(
            qw_h.at[pl.ds(pl.multiple_of(c * BASE + PAIR * i, 128), PAIR)], wq.at[i], w_sem.at[i]
        )
        for i in range(NP)
    ] + [pltpu.make_async_copy(qw_h.at[pl.ds(MID, 128)], wm, w_sem.at[NP])]
    for cp in w_loads:
        cp.start()

    partners = (
        [dev(dx, 0, 0, k) for dx in range(1, NX) for k in (c, oc)]
        + [dev(0, dy, 0, c) for dy in range(1, NY)]
        + [dev(0, 0, 1, c), dev(0, 0, NZ - 1, c), dev(0, 0, 0, oc)]
    )
    barrier = pltpu.get_barrier_semaphore()
    for who in partners:
        pl.semaphore_signal(barrier, inc=1, device_id=who, device_id_type=MESH)

    own_row = pl.multiple_of((c * NY + y) * TOK, TOK)

    def slope(q):
        def rows(r, carry):
            at_r = pl.ds(pl.multiple_of(r * 16, 16), 16)
            cols = pl.ds(q * FQ, FQ)
            g = grad[at_r, cols].astype(F32) * gelu_slope(pre[at_r, cols].astype(F32))
            gb[pl.ds(pl.multiple_of(own_row + r * 16, 16), 16), cols] = g.astype(BF16)
            return carry

        lax.fori_loop(0, TOK // 16, rows, 0)

    def send_slope(q):
        block = gb.at[pl.ds(own_row, TOK), pl.ds(q * FQ, FQ)]
        for dy in (1, 3, 2):
            remote(block, block, g_send.at[q], g_recv.at[q], dev(0, dy, 0, c))

    def forward_slope(q):
        wait(gb.at[pl.ds(0, 3 * TOK), pl.ds(q * FQ, FQ)], g_recv.at[q])
        layer = gb.at[pl.ds(pl.multiple_of(c * NY * TOK, TOK), NY * TOK), pl.ds(q * FQ, FQ)]
        remote(layer, layer, f_send.at[q], f_recv.at[q], dev(0, 0, 0, oc))

    def wait_slope(q):
        wait(gb.at[pl.ds(0, NY * TOK), pl.ds(q * FQ, FQ)], f_recv.at[q])

    lanes = pl.ds(pl.multiple_of((c * NX + x) * TOK, TOK), TOK)

    def send_acts(d):
        for par in (0, 1):
            core = c if par == 0 else oc
            p = 2 * lax.rem(z + d, NZ) + core
            block = at32[pl.ds(pl.multiple_of(p * CH, 8), CH), :].astype(BF16)
            slot = 2 * d + par
            asend[slot] = block
            if par == 0:
                at[d, :, lanes] = block
            for dx in (1, 3, 2):
                remote(
                    asend.at[slot], at.at[d, :, lanes], a_send.at[d], a_recv.at[d], dev(dx, 0, 0, core)
                )
            if par == 1:
                remote(asend.at[slot], at.at[d, :, lanes], a_send.at[d], a_recv.at[d], dev(0, 0, 0, oc))

    def wait_acts(d):
        wait(at.at[d, :, pl.ds(0, 7 * TOK)], a_recv.at[d])

    def part(d, q):
        return lax.dot_general(
            at[d % NZ], gb[:, pl.ds(q * FQ, FQ)], (((1,), (0,)), ((), ())),
            preferred_element_type=F32,
        )

    def slot_of(r, q):
        return r * 4 + q if r < 3 else 12 + q % 2

    def ring(way, r, q):
        long = (q < 2) == (way == 0)
        offset = (4 if long else 3) - r
        if offset == 0:
            return
        d = offset if way == 0 else -offset
        mine = part(d, q)
        s = slot_of(r, q)
        if r == 0:
            src = zs.at[way, q]
        else:
            came = slot_of(r - 1, q)
            src = zr.at[way, came]
            wait(src, z_recv.at[way, came])
            mine = mine + src[...].astype(F32)
        src[...] = mine.astype(BF16)
        remote(
            src, zr.at[way, s], z_send.at[way, s], z_recv.at[way, s],
            dev(0, 0, 1 if way == 0 else NZ - 1, c),
        )

    def last(q):
        total = part(0, q)
        for way in (0, 1):
            long = (q < 2) == (way == 0)
            s = slot_of(3 if long else 2, q)
            wait(zr.at[way, s], z_recv.at[way, s])
            total = total + zr[way, s].astype(F32)
        gwo[:, pl.ds(q * FQ, FQ)] = total.astype(BF16)

    nt = (((1,), (1,)), ((), ()))

    def rescale(ref, row):
        by = scale[pl.ds(row, 1), :]

        def rows(r, carry):
            at_r = pl.ds(pl.multiple_of(r * 16, 16), 16)
            ref[at_r, :] = (ref[at_r, :].astype(F32) * by).astype(BF16)
            return carry

        lax.fori_loop(0, 8, rows, 0)

    def inputs(i):
        w_loads[i].wait()
        if i < NP:
            for h in (0, 1):
                rescale(wq.at[i, pl.ds(128 * h, 128)], c * 15 + 2 * i + h)
            for k in (0, 1):
                got = lax.dot_general(
                    gb[pl.ds(k * NX * TOK, NX * TOK), :], wq[i], nt, preferred_element_type=F32
                )
                gis[i, k] = got.reshape(NX, TOK, PAIR).astype(BF16)
            for dx in (1, 3, 2):
                to = lax.rem(x + dx, NX)
                remote(
                    gis.at[i, :, to], gir.at[i, dx - 1], i_send.at[i], i_recv.at[i], dev(dx, 0, 0, c)
                )
        else:
            rescale(wm, 14)
            got = lax.dot_general(
                gb[pl.ds(pl.multiple_of(c * NX * TOK, TOK), NX * TOK), :], wm[...], nt,
                preferred_element_type=F32,
            )
            gism[...] = got.reshape(NX, TOK, 128).astype(BF16)
            for dx in (1, 3, 2):
                to = lax.rem(x + dx, NX)
                remote(gism.at[to], girm.at[dx - 1], i_send.at[i], i_recv.at[i], dev(dx, 0, 0, c))

    def inputs_done(i):
        if i < NP:
            wait(gir.at[i], i_recv.at[i])
            cols = pl.ds(pl.multiple_of(c * BASE + PAIR * i, 128), PAIR)

            def total(k):
                got = gis[i, pl.ds(k, 1), pl.ds(x, 1)].reshape(TOK, PAIR).astype(F32)
                for s in range(3):
                    got = got + gir[i, s, pl.ds(k, 1)].reshape(TOK, PAIR).astype(F32)
                return got.astype(BF16)

            gsx[i] = total(oc)
            remote(gsx.at[i], go.at[:, cols], s_send, s_recv, dev(0, 0, 0, oc))
            go[:, cols] = total(c)
        else:
            wait(girm, i_recv.at[i])
            got = gism[pl.ds(x, 1)].reshape(TOK, 128).astype(F32)
            for s in range(3):
                got = got + girm[s].astype(F32)
            go[:, pl.ds(MID, 128)] = got.astype(BF16)

    loads[0].wait()
    loads[1].wait()
    slope(0)
    pl.semaphore_wait(barrier, len(partners))
    send_slope(0)
    loads[2].wait()

    def turn(b, carry):
        at_b = pl.ds(pl.multiple_of(b * 128, 128), 128)
        at32[at_b, :] = acts[:, at_b].astype(F32).T
        return carry

    lax.fori_loop(0, DL // 128, turn, 0)
    send_acts(4)
    slope(1)
    send_slope(1)
    send_acts(5)
    send_acts(3)
    for q in (2, 3):
        slope(q)
        send_slope(q)
    for d in (2, 6, 1, 7, 0):
        send_acts(d)

    forward_slope(0)
    loads[3].wait()
    for q in range(4):
        wait_slope(q)
        if q == 0:
            wait_acts(4)
        if q == 2:
            wait_acts(3)
        if q < 2:
            ring(0, 0, q)
            if q == 0:
                wait_acts(5)
            ring(1, 0, q)
        else:
            ring(1, 0, q)
            ring(0, 0, q)
        if q < 3:
            forward_slope(q + 1)
    inputs(0)
    inputs(1)
    wait_acts(2)
    wait_acts(6)
    for q in range(4):
        for way in (0, 1):
            ring(way, 1, q)
        inputs(2 + q)
    wait_acts(1)
    wait_acts(7)
    for q in range(4):
        for way in (0, 1):
            ring(way, 2, q)
        if q < 2:
            inputs(6 + q)
    for i in (0, 1, 2):
        inputs_done(i)
    wait_acts(0)
    for q in (0, 1):
        ring(0, 3, q)
        ring(1, 3, q + 2)
    for i in (3, 4, 5, 6, 7):
        inputs_done(i)
    wait(go.at[:, pl.ds(0, MID)], s_recv)
    out_i = pltpu.make_async_copy(go, gi_h, out_sem.at[0])
    out_i.start()
    for q in range(4):
        last(q)
    out_w = pltpu.make_async_copy(gwo, gw_h, out_sem.at[1])
    out_w.start()

    for q in range(4):
        wait(gb.at[pl.ds(0, 3 * TOK), pl.ds(q * FQ, FQ)], g_send.at[q])
        wait(gb.at[pl.ds(0, NY * TOK), pl.ds(q * FQ, FQ)], f_send.at[q])
    for d in range(NZ):
        wait(at.at[d, :, pl.ds(0, 7 * TOK)], a_send.at[d])
    for way in (0, 1):
        for s in range(14):
            wait(zr.at[way, s], z_send.at[way, s])
    for i in range(NP):
        wait(gir.at[i], i_send.at[i])
    wait(girm, i_send.at[NP])
    wait(go.at[:, pl.ds(0, MID)], s_send)
    out_i.wait()
    out_w.wait()


def local(activations, pre_act, grad_act, quant_weight, block_scale):
    dma = pltpu.SemaphoreType.DMA
    hbm = pl.BlockSpec(memory_space=pl.ANY)
    return pl.pallas_call(
        kernel,
        out_shape=(
            jax.ShapeDtypeStruct((TOK, DL), BF16),
            jax.ShapeDtypeStruct((CH, FL), BF16),
        ),
        in_specs=[hbm] * 5,
        out_specs=(hbm, hbm),
        scratch_shapes=[
            pltpu.VMEM((TOK, DL), BF16),
            pltpu.VMEM((TOK, FL), BF16),
            pltpu.VMEM((TOK, FL), BF16),
            pltpu.VMEM((29, FL), F32),
            pltpu.VMEM((NP, PAIR, FL), BF16),
            pltpu.VMEM((128, FL), BF16),
            pltpu.VMEM((DL, TOK), F32),
            pltpu.VMEM((2 * NZ, CH, TOK), BF16),
            pltpu.VMEM((NZ, CH, 8 * TOK), BF16),
            pltpu.VMEM((8 * TOK, FL), BF16),
            pltpu.VMEM((2, 4, CH, FQ), BF16),
            pltpu.VMEM((2, 14, CH, FQ), BF16),
            pltpu.VMEM((NP, 2, NX, TOK, PAIR), BF16),
            pltpu.VMEM((NX, TOK, 128), BF16),
            pltpu.VMEM((NP, 3, 2, TOK, PAIR), BF16),
            pltpu.VMEM((3, TOK, 128), BF16),
            pltpu.VMEM((NP, TOK, PAIR), BF16),
            pltpu.VMEM((TOK, DL), BF16),
            pltpu.VMEM((CH, FL), BF16),
            dma((4,)), dma((NP + 1,)),
            dma((NZ,)), dma((NZ,)),
            dma((4,)), dma((4,)), dma((4,)), dma((4,)),
            dma((2, 14)), dma((2, 14)),
            dma((NP + 1,)), dma((NP + 1,)),
            dma, dma, dma((2,)),
        ],
        compiler_params=pltpu.CompilerParams(
            collective_id=0, has_side_effects=True, vmem_limit_bytes=56 * 2**20
        ),
        cost_estimate=pl.CostEstimate(
            flops=2 * 2 * 512 * FL * DL, bytes_accessed=20 * 2**20, transcendentals=2 * TOK * FL
        ),
    )(activations, pre_act, grad_act, quant_weight, block_scale)


def solution(mesh):
    placed = (
        P(("row", "depth"), "col"),
        P(("col", "depth"), "row"),
        P(("col", "depth"), "row"),
        P("col", "row"),
        P("col", "row"),
    )
    return jax.shard_map(
        local,
        mesh=mesh,
        in_specs=placed,
        out_specs=(P(("row", "depth"), "col"), P(("col", "depth"), "row")),
        check_vma=False,
    )
```

```python
import jax
import jax.numpy as jnp
from jax import lax
from jax.experimental import pallas as pl
from jax.experimental.pallas import tpu as pltpu
from jax.sharding import PartitionSpec as P

MESH = pl.DeviceIdType.MESH
BF16, F32 = jnp.bfloat16, jnp.float32
NX, NY, NZ = 4, 4, 8
TOK = 128
FL = 2048
DL = 3712
CH = 232
FQ = 512
SLICES = ((0, 256), (256, 256), (512, 256), (768, 256), (1024, 512), (1536, 512))
NS = len(SLICES)
DIRECT = (4, 5, 3)
WIN = 640
PAIR = 256
NP = 7
BASE = 1920
MID = 1792

inv_sqrt_two = 0.7071067811865476
inv_sqrt_tau = 0.3989422804014327


def gelu_slope(values):
    return (
        0.5 * (1.0 + lax.erf(values * inv_sqrt_two))
        + values * jnp.exp(-0.5 * values * values) * inv_sqrt_tau
    )


def kernel(
    acts_h, pre_h, grad_h, qw_h, scale_h, gi_h, gw_h,
    acts, pre, grad, scale, wq, wm, at32, asend, at, gb, zs, zr,
    gis, gism, gir, girm, gia, giam, gsx, go, gwo, own,
    in_sem, w_sem, a_send, a_recv, h_send, h_recv, g_send, g_recv, f_send, f_recv,
    z_send, z_recv, i_send, i_recv, j_send, j_recv, s_send, s_recv, out_sem,
):
    x, y, depth = lax.axis_index("row"), lax.axis_index("col"), lax.axis_index("depth")
    z, c = depth // 2, lax.rem(depth, 2)
    oc = 1 - c

    def dev(dx, dy, dz, core):
        return (
            lax.rem(x + dx, NX),
            lax.rem(y + dy, NY),
            lax.rem(z + dz, NZ) * 2 + core,
        )

    def remote(src, dst, send, recv, where):
        pltpu.make_async_remote_copy(
            src_ref=src, dst_ref=dst, send_sem=send, recv_sem=recv,
            device_id=where, device_id_type=MESH,
        ).start()

    def wait(ref, sem):
        pltpu.make_async_copy(ref, ref, sem).wait()

    head, tail = pl.ds(*SLICES[0]), pl.ds(SLICES[1][0], FL - SLICES[1][0])
    loads = [
        pltpu.make_async_copy(pre_h.at[:, head], pre.at[:, head], in_sem.at[0]),
        pltpu.make_async_copy(grad_h.at[:, head], grad.at[:, head], in_sem.at[1]),
        pltpu.make_async_copy(acts_h, acts, in_sem.at[2]),
        pltpu.make_async_copy(pre_h.at[:, tail], pre.at[:, tail], in_sem.at[3]),
        pltpu.make_async_copy(grad_h.at[:, tail], grad.at[:, tail], in_sem.at[4]),
        pltpu.make_async_copy(scale_h, scale, in_sem.at[5]),
    ]
    for cp in loads[:5]:
        cp.start()
    w_loads = [
        pltpu.make_async_copy(
            qw_h.at[pl.ds(pl.multiple_of(c * BASE + PAIR * i, 128), PAIR)], wq.at[i], w_sem.at[i]
        )
        for i in range(NP)
    ] + [pltpu.make_async_copy(qw_h.at[pl.ds(MID, 128)], wm, w_sem.at[NP])]

    partners = (
        [dev(dx, 0, 0, k) for dx in range(1, NX) for k in (c, oc)]
        + [dev(0, dy, 0, c) for dy in range(1, NY)]
        + [dev(0, 0, 1, c), dev(0, 0, NZ - 1, c), dev(0, 0, 0, oc)]
    )
    barrier = pltpu.get_barrier_semaphore()
    for who in partners:
        pl.semaphore_signal(barrier, inc=1, device_id=who, device_id_type=MESH)

    own_row = pl.multiple_of((c * NY + y) * TOK, TOK)

    def hidden(q):
        return pl.ds(*SLICES[q])

    def slope(q):
        def rows(r, carry):
            at_r = pl.ds(pl.multiple_of(r * 16, 16), 16)
            cols = hidden(q)
            g = grad[at_r, cols].astype(F32) * gelu_slope(pre[at_r, cols].astype(F32))
            gb[pl.ds(pl.multiple_of(own_row + r * 16, 16), 16), cols] = g.astype(BF16)
            return carry

        lax.fori_loop(0, TOK // 16, rows, 0)

    def send_slope(q):
        block = gb.at[pl.ds(own_row, TOK), hidden(q)]
        for dy in (1, 3, 2):
            remote(block, block, g_send.at[q], g_recv.at[q], dev(0, dy, 0, c))

    def forward_slope(q):
        wait(gb.at[pl.ds(0, 3 * TOK), hidden(q)], g_recv.at[q])
        layer = gb.at[pl.ds(pl.multiple_of(c * NY * TOK, TOK), NY * TOK), hidden(q)]
        remote(layer, layer, f_send.at[q], f_recv.at[q], dev(0, 0, 0, oc))

    def wait_slope(q):
        wait(gb.at[pl.ds(0, NY * TOK), hidden(q)], f_recv.at[q])

    lanes = pl.ds(pl.multiple_of((c * NX + x) * TOK, TOK), TOK)

    def turn_acts(d):
        owner = lax.rem(z + d, NZ)
        tile = jnp.minimum(owner * (2 * CH) // 128, (DL - WIN) // 128)
        for i in range(WIN // 128):
            cols = pl.ds(pl.multiple_of((tile + i) * 128, 128), 128)
            at32[pl.ds(128 * i, 128), :] = acts[:, cols].astype(F32).T
        skip = owner * (2 * CH) - tile * 128
        for par in (0, 1):
            core = c if par == 0 else oc
            block = at32[pl.ds(pl.multiple_of(skip + core * CH, 8), CH), :].astype(BF16)
            asend[2 * d + par] = block
            if par == 0:
                at[d, :, lanes] = block

    def post_acts(d):
        for par in (0, 1):
            core = c if par == 0 else oc
            block = asend.at[2 * d + par]
            for dx in (1, 3, 2) if d in DIRECT else (1, 3):
                remote(block, at.at[d, :, lanes], a_send.at[d], a_recv.at[d], dev(dx, 0, 0, core))
            if par == 1:
                remote(block, at.at[d, :, lanes], a_send.at[d], a_recv.at[d], dev(0, 0, 0, oc))

    def send_acts(d):
        turn_acts(d)
        post_acts(d)

    def hand_on(d):
        wait(at.at[d, :, pl.ds(0, 5 * TOK)], a_recv.at[d])
        for dx, core in ((1, c), (3, oc)):
            block = at.at[
                d, :, pl.ds(pl.multiple_of((core * NX + lax.rem(x - dx + NX, NX)) * TOK, TOK), TOK)
            ]
            remote(block, block, h_send.at[d], h_recv.at[d], dev(dx, 0, 0, c))

    def wait_acts(d):
        if d in DIRECT:
            wait(at.at[d, :, pl.ds(0, 7 * TOK)], a_recv.at[d])
        else:
            wait(at.at[d, :, pl.ds(0, 2 * TOK)], h_recv.at[d])

    def part(d, q):
        return lax.dot_general(
            at[d % NZ], gb[:, hidden(q)], (((1,), (0,)), ((), ())),
            preferred_element_type=F32,
        )

    def is_long(way, q):
        return q % 2 == way

    def landing(way, r, q):
        return zr.at[way, r, :, hidden(q)]

    def ring(way, r, q):
        offset = (4 if is_long(way, q) else 3) - r
        if offset == 0:
            return
        mine = part(offset if way == 0 else -offset, q)
        if r == 0:
            src = zs.at[way, :, hidden(q)]
        else:
            src = landing(way, r - 1, q)
            wait(src, z_recv.at[way, r - 1, q])
            mine = mine + src[...].astype(F32)
        src[...] = mine.astype(BF16)
        remote(
            src, landing(way, r, q), z_send.at[way, r, q], z_recv.at[way, r, q],
            dev(0, 0, 1 if way == 0 else NZ - 1, c),
        )

    def add_short(q):
        way = 1 if is_long(0, q) else 0
        total = part(0, q)
        wait(landing(way, 2, q), z_recv.at[way, 2, q])
        own[:, hidden(q)] = total + landing(way, 2, q)[...].astype(F32)

    def add_long(q):
        way = 0 if is_long(0, q) else 1
        wait(landing(way, 3, q), z_recv.at[way, 3, q])
        gwo[:, hidden(q)] = (own[:, hidden(q)] + landing(way, 3, q)[...].astype(F32)).astype(BF16)
        pltpu.make_async_copy(
            gwo.at[:, hidden(q)], gw_h.at[:, hidden(q)], out_sem.at[1 + q]
        ).start()

    nt = (((1,), (1,)), ((), ()))

    def rescale(ref, row):
        by = scale[pl.ds(row, 1), :]

        def rows(r, carry):
            at_r = pl.ds(pl.multiple_of(r * 16, 16), 16)
            ref[at_r, :] = (ref[at_r, :].astype(F32) * by).astype(BF16)
            return carry

        lax.fori_loop(0, 8, rows, 0)

    def inputs(i):
        w_loads[i].wait()
        if i < NP:
            for h in (0, 1):
                rescale(wq.at[i, pl.ds(128 * h, 128)], c * 15 + 2 * i + h)
            for k in (0, 1):
                got = lax.dot_general(
                    gb[pl.ds(k * NX * TOK, NX * TOK), :], wq[i], nt, preferred_element_type=F32
                )
                gis[i, k] = got.reshape(NX, TOK, PAIR).astype(BF16)
            far = lax.rem(x + 2, NX)
            for k, dx in ((0, 1), (1, 3)):
                remote(
                    gis.at[i, k, far], gia.at[i, k], j_send.at[i], j_recv.at[i], dev(dx, 0, 0, c)
                )
        else:
            rescale(wm, 14)
            got = lax.dot_general(
                gb[pl.ds(pl.multiple_of(c * NX * TOK, TOK), NX * TOK), :], wm[...], nt,
                preferred_element_type=F32,
            )
            gism[...] = got.reshape(NX, TOK, 128).astype(BF16)
            far = lax.rem(x + 2, NX)
            for k, dx in ((0, 1), (1, 3)):
                remote(
                    gism.at[far, pl.ds(64 * k, 64)], giam.at[k], j_send.at[i], j_recv.at[i],
                    dev(dx, 0, 0, c),
                )

    def inputs_on(i):
        wait(gia.at[i] if i < NP else giam, j_recv.at[i])
        for k, dx in ((0, 1), (1, 3)):
            to = lax.rem(x + dx, NX)
            if i < NP:
                mine, came = gis.at[i, k, to], gia.at[i, k]
            else:
                mine, came = gism.at[to, pl.ds(64 * k, 64)], giam.at[k]
            mine[...] = (mine[...].astype(F32) + came[...].astype(F32)).astype(BF16)
            if i < NP:
                remote(gis.at[i, :, to], gir.at[i, k], i_send.at[i], i_recv.at[i], dev(dx, 0, 0, c))
            else:
                remote(gism.at[to], girm.at[k], i_send.at[i], i_recv.at[i], dev(dx, 0, 0, c))

    def inputs_done(i):
        if i < NP:
            wait(gir.at[i], i_recv.at[i])
            cols = pl.ds(pl.multiple_of(c * BASE + PAIR * i, 128), PAIR)

            def total(k):
                got = gis[i, pl.ds(k, 1), pl.ds(x, 1)].reshape(TOK, PAIR).astype(F32)
                for s in range(2):
                    got = got + gir[i, s, pl.ds(k, 1)].reshape(TOK, PAIR).astype(F32)
                return got.astype(BF16)

            gsx[i] = total(oc)
            remote(gsx.at[i], go.at[:, cols], s_send, s_recv, dev(0, 0, 0, oc))
            go[:, cols] = total(c)
        else:
            wait(girm, i_recv.at[i])
            got = gism[pl.ds(x, 1)].reshape(TOK, 128).astype(F32)
            for s in range(2):
                got = got + girm[s].astype(F32)
            go[:, pl.ds(MID, 128)] = got.astype(BF16)

    handed, here = set(), set()

    def step(way, r, q):
        offset = (4 if is_long(way, q) else 3) - r
        d = (offset if way == 0 else -offset) % NZ
        if d not in here:
            if d not in DIRECT and d not in handed:
                hand_on(d)
                handed.add(d)
            wait_acts(d)
            here.add(d)
        ring(way, r, q)

    def first_half(q):
        forward_slope(q)
        if q + 2 < NS:
            send_slope(q + 2)

    def pass_on(d):
        hand_on(d)
        handed.add(d)

    loads[2].wait()
    turn_acts(4)
    loads[0].wait()
    loads[1].wait()
    slope(0)
    pl.semaphore_wait(barrier, len(partners))
    send_slope(0)
    post_acts(4)
    loads[3].wait()
    loads[4].wait()
    slope(1)
    send_slope(1)
    for cp in [loads[5]] + w_loads:
        cp.start()
    slope(2)
    slope(3)

    plan = (
        ("F0 A5 W0 000", "S4 F1 A3 W1", "101 S5 F2 W2", "002 100 F3 A6", "W3 103 001 102")
        + ("010 111", "F4 A2 W4 004", "003 104", "F5 A7 W5 105", "005 H6")
        + ("I0 A1 012 113", "H2 I1 110 011", "A0 I2 014 115", "J0 H7 I3", "112 013 J1 I4")
        + ("020 121 H1", "J2 I5 114 015", "H0 J3 I6", "022 123 J4", "I7 120 021 024", "J5 125")
        + ("J6 D0 030 131", "J7 D1 122 023", "D2 032 133", "D3 124 025", "D4 034 135", "D5")
    )
    does = dict(
        F=first_half, A=send_acts, W=wait_slope, H=pass_on, S=slope,
        I=inputs, J=inputs_on, D=inputs_done,
    )
    for word in " ".join(plan).split():
        if word == "I0":
            loads[5].wait()
        if word[0] in does:
            does[word[0]](int(word[1:]))
        else:
            step(*map(int, word))
    if 0 not in here:
        wait_acts(0)
    for q in range(NS):
        add_short(q)
    inputs_done(6)
    inputs_done(7)
    wait(go.at[:, pl.ds(0, MID)], s_recv)
    out_i = pltpu.make_async_copy(go, gi_h, out_sem.at[0])
    out_i.start()
    for q in range(NS):
        add_long(q)

    for q in range(NS):
        wait(gb.at[pl.ds(0, 3 * TOK), hidden(q)], g_send.at[q])
        wait(gb.at[pl.ds(0, NY * TOK), hidden(q)], f_send.at[q])
    for d in range(NZ):
        wait(at.at[d, :, pl.ds(0, (7 if d in DIRECT else 5) * TOK)], a_send.at[d])
        if d not in DIRECT:
            wait(at.at[d, :, pl.ds(0, 2 * TOK)], h_send.at[d])
    for way in (0, 1):
        for q in range(NS):
            for r in range(4 if is_long(way, q) else 3):
                wait(landing(way, r, q), z_send.at[way, r, q])
    for i in range(NP):
        wait(gia.at[i], j_send.at[i])
        wait(gir.at[i], i_send.at[i])
    wait(giam, j_send.at[NP])
    wait(girm, i_send.at[NP])
    wait(go.at[:, pl.ds(0, MID)], s_send)
    out_i.wait()
    for q in range(NS):
        wait(gwo.at[:, hidden(q)], out_sem.at[1 + q])


def copy_out(gi_in, gw_in, gi_out, gw_out, gi, gw, sem):
    pieces = [(pl.ds(32 * i, 32), slice(None)) for i in range(4)]
    bands = [(slice(None), pl.ds(FQ * i, FQ)) for i in range(4)]
    steps = [(gi_in.at[k], gi.at[k], gi_out.at[k]) for k in pieces] + [
        (gw_in.at[k], gw.at[k], gw_out.at[k]) for k in bands
    ]
    into = [pltpu.make_async_copy(src, mid, sem.at[0, i]) for i, (src, mid, _) in enumerate(steps)]
    out = [pltpu.make_async_copy(mid, dst, sem.at[1, i]) for i, (_, mid, dst) in enumerate(steps)]
    for cp in into:
        cp.start()
    for one, two in zip(into, out):
        one.wait()
        two.start()
    for cp in out:
        cp.wait()


def local(activations, pre_act, grad_act, quant_weight, block_scale):
    dma = pltpu.SemaphoreType.DMA
    hbm = pl.BlockSpec(memory_space=pl.ANY)
    shapes = (
        jax.ShapeDtypeStruct((TOK, DL), BF16),
        jax.ShapeDtypeStruct((CH, FL), BF16),
    )
    outs = pl.pallas_call(
        kernel,
        out_shape=shapes,
        in_specs=[hbm] * 5,
        out_specs=(hbm, hbm),
        scratch_shapes=[
            pltpu.VMEM((TOK, DL), BF16),
            pltpu.VMEM((TOK, FL), BF16),
            pltpu.VMEM((TOK, FL), BF16),
            pltpu.VMEM((29, FL), F32),
            pltpu.VMEM((NP, PAIR, FL), BF16),
            pltpu.VMEM((128, FL), BF16),
            pltpu.VMEM((WIN, TOK), F32),
            pltpu.VMEM((2 * NZ, CH, TOK), BF16),
            pltpu.VMEM((NZ, CH, 8 * TOK), BF16),
            pltpu.VMEM((8 * TOK, FL), BF16),
            pltpu.VMEM((2, CH, FL), BF16),
            pltpu.VMEM((2, 4, CH, FL), BF16),
            pltpu.VMEM((NP, 2, NX, TOK, PAIR), BF16),
            pltpu.VMEM((NX, TOK, 128), BF16),
            pltpu.VMEM((NP, 2, 2, TOK, PAIR), BF16),
            pltpu.VMEM((2, TOK, 128), BF16),
            pltpu.VMEM((NP, 2, TOK, PAIR), BF16),
            pltpu.VMEM((2, 64, 128), BF16),
            pltpu.VMEM((NP, TOK, PAIR), BF16),
            pltpu.VMEM((TOK, DL), BF16),
            pltpu.VMEM((CH, FL), BF16),
            pltpu.VMEM((CH, FL), F32),
            dma((6,)), dma((NP + 1,)),
            dma((NZ,)), dma((NZ,)), dma((NZ,)), dma((NZ,)),
            dma((NS,)), dma((NS,)), dma((NS,)), dma((NS,)),
            dma((2, 4, NS)), dma((2, 4, NS)),
            dma((NP + 1,)), dma((NP + 1,)), dma((NP + 1,)), dma((NP + 1,)),
            dma, dma,
            dma((1 + NS,)),
        ],
        compiler_params=pltpu.CompilerParams(
            collective_id=0, has_side_effects=True, vmem_limit_bytes=56 * 2**20
        ),
        cost_estimate=pl.CostEstimate(
            flops=2 * 2 * 512 * FL * DL, bytes_accessed=20 * 2**20, transcendentals=2 * TOK * FL
        ),
    )(activations, pre_act, grad_act, quant_weight, block_scale)
    return pl.pallas_call(
        copy_out,
        out_shape=shapes,
        in_specs=[hbm] * 2,
        out_specs=(hbm, hbm),
        scratch_shapes=[pltpu.VMEM((TOK, DL), BF16), pltpu.VMEM((CH, FL), BF16), dma((2, 8))],
    )(*outs)


def solution(mesh):
    placed = (
        P(("row", "depth"), "col"),
        P(("col", "depth"), "row"),
        P(("col", "depth"), "row"),
        P("col", "row"),
        P("col", "row"),
    )
    return jax.shard_map(
        local,
        mesh=mesh,
        in_specs=placed,
        out_specs=(P(("row", "depth"), "col"), P(("col", "depth"), "row")),
        check_vma=False,
    )
```

```python
import jax
import jax.numpy as jnp
from jax import lax
from jax.experimental import pallas as pl
from jax.experimental.pallas import tpu as pltpu
from jax.sharding import PartitionSpec as P

MESH = pl.DeviceIdType.MESH
BF16, F32 = jnp.bfloat16, jnp.float32
NX, NY, NZ = 4, 4, 8
TOK = 128
FL = 2048
DL = 3712
CH = 232
FQ = 512
SLICES = ((0, 256), (256, 256), (512, 256), (768, 256), (1024, 512), (1536, 512))
NS = len(SLICES)
DIRECT = ()
WIN = 640
PAIR = 256
NP = 7
BASE = 1920
MID = 1792

inv_sqrt_two = 0.7071067811865476
inv_sqrt_tau = 0.3989422804014327


def gelu_slope(values):
    return (
        0.5 * (1.0 + lax.erf(values * inv_sqrt_two))
        + values * jnp.exp(-0.5 * values * values) * inv_sqrt_tau
    )


def kernel(
    acts_h, pre_h, grad_h, qw_h, scale_h, gi_h, gw_h,
    acts, pre, grad, scale, wq, wm, at32, asend, at, gb, zs, zr,
    gis, gism, gir, girm, gia, giam, gsx, go, gwo, own,
    in_sem, w_sem, a_send, a_recv, h_send, h_recv, g_send, g_recv, f_send, f_recv,
    z_send, z_recv, i_send, i_recv, j_send, j_recv, s_send, s_recv,
    n_send, n_recv, m_send, m_recv, out_sem,
):
    x, y, depth = lax.axis_index("row"), lax.axis_index("col"), lax.axis_index("depth")
    z, c = depth // 2, lax.rem(depth, 2)
    oc = 1 - c

    def dev(dx, dy, dz, core):
        return (
            lax.rem(x + dx, NX),
            lax.rem(y + dy, NY),
            lax.rem(z + dz, NZ) * 2 + core,
        )

    def remote(src, dst, send, recv, where):
        pltpu.make_async_remote_copy(
            src_ref=src, dst_ref=dst, send_sem=send, recv_sem=recv,
            device_id=where, device_id_type=MESH,
        ).start()

    def wait(ref, sem):
        pltpu.make_async_copy(ref, ref, sem).wait()

    head, tail = pl.ds(*SLICES[0]), pl.ds(SLICES[1][0], FL - SLICES[1][0])
    loads = [
        pltpu.make_async_copy(pre_h.at[:, head], pre.at[:, head], in_sem.at[0]),
        pltpu.make_async_copy(grad_h.at[:, head], grad.at[:, head], in_sem.at[1]),
        pltpu.make_async_copy(acts_h, acts, in_sem.at[2]),
        pltpu.make_async_copy(pre_h.at[:, tail], pre.at[:, tail], in_sem.at[3]),
        pltpu.make_async_copy(grad_h.at[:, tail], grad.at[:, tail], in_sem.at[4]),
        pltpu.make_async_copy(scale_h, scale, in_sem.at[5]),
    ]
    for cp in loads[:5]:
        cp.start()
    w_loads = [
        pltpu.make_async_copy(
            qw_h.at[pl.ds(pl.multiple_of(c * BASE + PAIR * i, 128), PAIR)], wq.at[i], w_sem.at[i]
        )
        for i in range(NP)
    ] + [pltpu.make_async_copy(qw_h.at[pl.ds(MID, 128)], wm, w_sem.at[NP])]

    partners = (
        [dev(dx, 0, 0, k) for dx in range(1, NX) for k in (c, oc)]
        + [dev(0, dy, 0, c) for dy in range(1, NY)]
        + [dev(0, 0, 1, c), dev(0, 0, NZ - 1, c), dev(0, 0, 0, oc)]
    )
    barrier = pltpu.get_barrier_semaphore()
    for who in partners:
        pl.semaphore_signal(barrier, inc=1, device_id=who, device_id_type=MESH)

    own_row = pl.multiple_of((c * NY + y) * TOK, TOK)

    def hidden(q):
        first, units = SLICES[q % NS]
        return pl.ds(first + q // NS * FL, units)

    def ship_slope(q):
        own = pl.ds(own_row, TOK)
        remote(
            gb.at[own, hidden(q)], gb.at[own, hidden(NS + q)], n_send.at[q], n_recv.at[q],
            dev(0, 0, NZ - 1 if q % 2 else 1, c),
        )

    def take_slope(q):
        wait(gb.at[pl.ds(0, TOK), hidden(q)], n_recv.at[q - NS])

    def slope(q):
        def rows(r, carry):
            at_r = pl.ds(pl.multiple_of(r * 16, 16), 16)
            cols = hidden(q)
            g = grad[at_r, cols].astype(F32) * gelu_slope(pre[at_r, cols].astype(F32))
            gb[pl.ds(pl.multiple_of(own_row + r * 16, 16), 16), cols] = g.astype(BF16)
            return carry

        lax.fori_loop(0, TOK // 16, rows, 0)

    def send_slope(q):
        block = gb.at[pl.ds(own_row, TOK), hidden(q)]
        for dy in (1, 3, 2):
            remote(block, block, g_send.at[q], g_recv.at[q], dev(0, dy, 0, c))

    def forward_slope(q):
        wait(gb.at[pl.ds(0, 3 * TOK), hidden(q)], g_recv.at[q])
        layer = gb.at[pl.ds(pl.multiple_of(c * NY * TOK, TOK), NY * TOK), hidden(q)]
        remote(layer, layer, f_send.at[q], f_recv.at[q], dev(0, 0, 0, oc))

    def wait_slope(q):
        wait(gb.at[pl.ds(0, NY * TOK), hidden(q)], f_recv.at[q])

    lanes = pl.ds(pl.multiple_of((c * NX + x) * TOK, TOK), TOK)

    def turn_acts(d):
        owner = lax.rem(z + d, NZ)
        tile = jnp.minimum(owner * (2 * CH) // 128, (DL - WIN) // 128)
        for i in range(WIN // 128):
            cols = pl.ds(pl.multiple_of((tile + i) * 128, 128), 128)
            at32[pl.ds(128 * i, 128), :] = acts[:, cols].astype(F32).T
        skip = owner * (2 * CH) - tile * 128
        for par in (0, 1):
            core = c if par == 0 else oc
            block = at32[pl.ds(pl.multiple_of(skip + core * CH, 8), CH), :].astype(BF16)
            asend[2 * d + par] = block
            if par == 0:
                at[d, :, lanes] = block

    def post_acts(d):
        for par in (0, 1):
            core = c if par == 0 else oc
            block = asend.at[2 * d + par]
            for dx in (1, 3, 2) if d in DIRECT else (1, 3):
                remote(block, at.at[d, :, lanes], a_send.at[d], a_recv.at[d], dev(dx, 0, 0, core))
            if par == 1:
                remote(block, at.at[d, :, lanes], a_send.at[d], a_recv.at[d], dev(0, 0, 0, oc))

    def send_acts(d):
        turn_acts(d)
        post_acts(d)

    def ship_acts():
        for way in (0, 1):
            for par in (0, 1):
                remote(
                    asend.at[8 + par], asend.at[2 * (NZ + way) + par], m_send.at[way, par],
                    m_recv.at[way, par], dev(0, 0, 1 if way == 0 else NZ - 1, c),
                )

    def take_acts(d):
        for par in (0, 1):
            wait(asend.at[2 * d + par], m_recv.at[d - NZ, par])
        at[d, :, lanes] = asend[2 * d]
        post_acts(d)

    def hand_on(d):
        wait(at.at[d, :, pl.ds(0, 5 * TOK)], a_recv.at[d])
        for dx, core in ((1, c), (3, oc)):
            block = at.at[
                d, :, pl.ds(pl.multiple_of((core * NX + lax.rem(x - dx + NX, NX)) * TOK, TOK), TOK)
            ]
            remote(block, block, h_send.at[d], h_recv.at[d], dev(dx, 0, 0, c))

    def wait_acts(d):
        if d in DIRECT:
            wait(at.at[d, :, pl.ds(0, 7 * TOK)], a_recv.at[d])
        else:
            wait(at.at[d, :, pl.ds(0, 2 * TOK)], h_recv.at[d])

    def part(d, q):
        return lax.dot_general(
            at[d], gb[:, hidden(q)], (((1,), (0,)), ((), ())),
            preferred_element_type=F32,
        )

    def is_long(way, q):
        return q % 2 == way

    def landing(way, r, q):
        return zr.at[way, r, :, hidden(q)]

    def ring(way, r, q):
        long = is_long(way, q)
        offset = (4 if long else 3) - r
        mine = part(offset if way == 0 else NZ - offset, q)
        if r == 0 or (long and r == 1):
            src = zs.at[way, :, hidden(q)]
            if long:
                mine = mine + part(NZ + way, NS + q)
        else:
            src = landing(way, r - 1, q)
            wait(src, z_recv.at[way, r - 1, q])
            mine = mine + src[...].astype(F32)
        src[...] = mine.astype(BF16)
        remote(
            src, landing(way, r, q), z_send.at[way, r, q], z_recv.at[way, r, q],
            dev(0, 0, 1 if way == 0 else NZ - 1, c),
        )

    def add_short(q):
        way = 1 if is_long(0, q) else 0
        total = part(0, q)
        wait(landing(way, 2, q), z_recv.at[way, 2, q])
        own[:, hidden(q)] = total + landing(way, 2, q)[...].astype(F32)

    def add_long(q):
        way = 0 if is_long(0, q) else 1
        wait(landing(way, 3, q), z_recv.at[way, 3, q])
        gwo[:, hidden(q)] = (own[:, hidden(q)] + landing(way, 3, q)[...].astype(F32)).astype(BF16)
        pltpu.make_async_copy(
            gwo.at[:, hidden(q)], gw_h.at[:, hidden(q)], out_sem.at[1 + q]
        ).start()

    nt = (((1,), (1,)), ((), ()))

    def rescale(ref, row):
        by = scale[pl.ds(row, 1), :]

        def rows(r, carry):
            at_r = pl.ds(pl.multiple_of(r * 16, 16), 16)
            ref[at_r, :] = (ref[at_r, :].astype(F32) * by).astype(BF16)
            return carry

        lax.fori_loop(0, 8, rows, 0)

    def inputs(i):
        w_loads[i].wait()
        if i < NP:
            for h in (0, 1):
                rescale(wq.at[i, pl.ds(128 * h, 128)], c * 15 + 2 * i + h)
            for k in (0, 1):
                got = lax.dot_general(
                    gb[pl.ds(k * NX * TOK, NX * TOK), pl.ds(0, FL)], wq[i], nt, preferred_element_type=F32
                )
                gis[i, k] = got.reshape(NX, TOK, PAIR).astype(BF16)
            far = lax.rem(x + 2, NX)
            for k, dx in ((0, 1), (1, 3)):
                remote(
                    gis.at[i, k, far], gia.at[i, k], j_send.at[i], j_recv.at[i], dev(dx, 0, 0, c)
                )
        else:
            rescale(wm, 14)
            got = lax.dot_general(
                gb[pl.ds(pl.multiple_of(c * NX * TOK, TOK), NX * TOK), pl.ds(0, FL)], wm[...], nt,
                preferred_element_type=F32,
            )
            gism[...] = got.reshape(NX, TOK, 128).astype(BF16)
            far = lax.rem(x + 2, NX)
            for k, dx in ((0, 1), (1, 3)):
                remote(
                    gism.at[far, pl.ds(64 * k, 64)], giam.at[k], j_send.at[i], j_recv.at[i],
                    dev(dx, 0, 0, c),
                )

    def inputs_on(i):
        wait(gia.at[i] if i < NP else giam, j_recv.at[i])
        for k, dx in ((0, 1), (1, 3)):
            to = lax.rem(x + dx, NX)
            if i < NP:
                mine, came = gis.at[i, k, to], gia.at[i, k]
            else:
                mine, came = gism.at[to, pl.ds(64 * k, 64)], giam.at[k]
            mine[...] = (mine[...].astype(F32) + came[...].astype(F32)).astype(BF16)
            if i < NP:
                remote(gis.at[i, :, to], gir.at[i, k], i_send.at[i], i_recv.at[i], dev(dx, 0, 0, c))
            else:
                remote(gism.at[to], girm.at[k], i_send.at[i], i_recv.at[i], dev(dx, 0, 0, c))

    def inputs_done(i):
        if i < NP:
            wait(gir.at[i], i_recv.at[i])
            cols = pl.ds(pl.multiple_of(c * BASE + PAIR * i, 128), PAIR)

            def total(k):
                got = gis[i, pl.ds(k, 1), pl.ds(x, 1)].reshape(TOK, PAIR).astype(F32)
                for s in range(2):
                    got = got + gir[i, s, pl.ds(k, 1)].reshape(TOK, PAIR).astype(F32)
                return got.astype(BF16)

            gsx[i] = total(oc)
            remote(gsx.at[i], go.at[:, cols], s_send, s_recv, dev(0, 0, 0, oc))
            go[:, cols] = total(c)
        else:
            wait(girm, i_recv.at[i])
            got = gism[pl.ds(x, 1)].reshape(TOK, 128).astype(F32)
            for s in range(2):
                got = got + girm[s].astype(F32)
            go[:, pl.ds(MID, 128)] = got.astype(BF16)

    handed, here, summed, scaled = set(), set(), set(), False

    def get(d):
        if d not in here:
            if d not in DIRECT:
                pass_on(d)
            wait_acts(d)
            here.add(d)

    def step(way, r, q):
        offset = (4 if is_long(way, q) else 3) - r
        get(offset if way == 0 else NZ - offset)
        if r == 1 and is_long(way, q):
            get(NZ + way)
        ring(way, r, q)

    def pass_on(d):
        if d not in handed:
            hand_on(d)
            handed.add(d)

    def spread(q):
        take_slope(q)
        send_slope(q)

    def own_slice(q):
        slope(q)
        ship_slope(q)

    loads[2].wait()
    turn_acts(4)
    loads[0].wait()
    loads[1].wait()
    slope(0)
    pl.semaphore_wait(barrier, len(partners))
    send_slope(0)
    ship_acts()
    ship_slope(0)
    send_acts(5)
    loads[3].wait()
    loads[4].wait()
    own_slice(1)
    send_slope(1)
    send_acts(3)
    for cp in [loads[5]] + w_loads:
        cp.start()

    plan = (
        ("S3 S2 G2 G3", "F0 S4 H5 G4", "W0 A6 F1 H3", "S5 G5 100 F2", "A2 U6 H6 W2",)
        + ("U7 102 F3 W1", "001 U8 A7 W3", "003 H2 U9 U10", "U11 110 A1 F4", "112 H7 T8 013",)
        + ("011 W4 104 T9", "H1 F5 A0 122", "120 W5 005 I4", "F7 H9 F6 114", "023 021 H8 W6",)
        + ("F8 I0 H0 015", "F9 J4 W8 I2", "012 010 W9 113", "J0 124 F10 I5", "D4 J2 W10 014",)
        + ("025 D0 F11 123", "022 J5 I1 020", "D2 W11 115 133", "D5 I3 024 J1", "I6 J3 W7 111",)
        + ("125 I7 D1 J6", "032 121 D3 J7", "030 D6 D7 135", "034 131",)
    )
    does = dict(
        F=forward_slope, A=send_acts, W=wait_slope, H=pass_on, S=own_slice,
        G=send_slope, T=take_acts, U=spread, I=inputs, J=inputs_on, D=inputs_done,
    )
    for word in " ".join(plan).split():
        if word[0] == "I" and not scaled:
            loads[5].wait()
            scaled = True
        if word[0] == "D":
            summed.add(int(word[1:]))
        if word[0] in does:
            does[word[0]](int(word[1:]))
        else:
            step(*map(int, word))
    if 0 not in here:
        wait_acts(0)
    for q in range(NS):
        add_short(q)
    for i in range(NP + 1):
        if i not in summed:
            inputs_done(i)
    wait(go.at[:, pl.ds(0, MID)], s_recv)
    out_i = pltpu.make_async_copy(go, gi_h, out_sem.at[0])
    out_i.start()
    for q in range(NS):
        add_long(q)

    for q in range(NS):
        wait(gb.at[pl.ds(0, 3 * TOK), hidden(q)], g_send.at[q])
        wait(gb.at[pl.ds(0, NY * TOK), hidden(q)], f_send.at[q])
    for q in range(NS, 2 * NS):
        wait(gb.at[pl.ds(0, 3 * TOK), hidden(q)], g_send.at[q])
        wait(gb.at[pl.ds(0, NY * TOK), hidden(q)], f_send.at[q])
        wait(gb.at[pl.ds(0, TOK), hidden(q)], n_send.at[q - NS])
    for way in (0, 1):
        for par in (0, 1):
            wait(asend.at[8 + par], m_send.at[way, par])
    for d in (0, 1, 2, 3, 5, 6, 7, 8, 9):
        wait(at.at[d, :, pl.ds(0, (7 if d in DIRECT else 5) * TOK)], a_send.at[d])
        if d not in DIRECT:
            wait(at.at[d, :, pl.ds(0, 2 * TOK)], h_send.at[d])
    for way in (0, 1):
        for q in range(NS):
            for r in range(1, 4) if is_long(way, q) else range(3):
                wait(landing(way, r, q), z_send.at[way, r, q])
    for i in range(NP):
        wait(gia.at[i], j_send.at[i])
        wait(gir.at[i], i_send.at[i])
    wait(giam, j_send.at[NP])
    wait(girm, i_send.at[NP])
    wait(go.at[:, pl.ds(0, MID)], s_send)
    out_i.wait()
    for q in range(NS):
        wait(gwo.at[:, hidden(q)], out_sem.at[1 + q])


def copy_out(gi_in, gw_in, gi_out, gw_out, gi, gw, sem):
    pieces = [(pl.ds(32 * i, 32), slice(None)) for i in range(4)]
    bands = [(slice(None), pl.ds(FQ * i, FQ)) for i in range(4)]
    steps = [(gi_in.at[k], gi.at[k], gi_out.at[k]) for k in pieces] + [
        (gw_in.at[k], gw.at[k], gw_out.at[k]) for k in bands
    ]
    into = [pltpu.make_async_copy(src, mid, sem.at[0, i]) for i, (src, mid, _) in enumerate(steps)]
    out = [pltpu.make_async_copy(mid, dst, sem.at[1, i]) for i, (_, mid, dst) in enumerate(steps)]
    for cp in into:
        cp.start()
    for one, two in zip(into, out):
        one.wait()
        two.start()
    for cp in out:
        cp.wait()


def local(activations, pre_act, grad_act, quant_weight, block_scale):
    dma = pltpu.SemaphoreType.DMA
    hbm = pl.BlockSpec(memory_space=pl.ANY)
    shapes = (
        jax.ShapeDtypeStruct((TOK, DL), BF16),
        jax.ShapeDtypeStruct((CH, FL), BF16),
    )
    outs = pl.pallas_call(
        kernel,
        out_shape=shapes,
        in_specs=[hbm] * 5,
        out_specs=(hbm, hbm),
        scratch_shapes=[
            pltpu.VMEM((TOK, DL), BF16),
            pltpu.VMEM((TOK, FL), BF16),
            pltpu.VMEM((TOK, FL), BF16),
            pltpu.VMEM((29, FL), F32),
            pltpu.VMEM((NP, PAIR, FL), BF16),
            pltpu.VMEM((128, FL), BF16),
            pltpu.VMEM((WIN, TOK), F32),
            pltpu.VMEM((2 * NZ + 4, CH, TOK), BF16),
            pltpu.VMEM((NZ + 2, CH, 8 * TOK), BF16),
            pltpu.VMEM((8 * TOK, 2 * FL), BF16),
            pltpu.VMEM((2, CH, FL), BF16),
            pltpu.VMEM((2, 4, CH, FL), BF16),
            pltpu.VMEM((NP, 2, NX, TOK, PAIR), BF16),
            pltpu.VMEM((NX, TOK, 128), BF16),
            pltpu.VMEM((NP, 2, 2, TOK, PAIR), BF16),
            pltpu.VMEM((2, TOK, 128), BF16),
            pltpu.VMEM((NP, 2, TOK, PAIR), BF16),
            pltpu.VMEM((2, 64, 128), BF16),
            pltpu.VMEM((NP, TOK, PAIR), BF16),
            pltpu.VMEM((TOK, DL), BF16),
            pltpu.VMEM((CH, FL), BF16),
            pltpu.VMEM((CH, FL), F32),
            dma((6,)), dma((NP + 1,)),
            dma((NZ + 2,)), dma((NZ + 2,)), dma((NZ + 2,)), dma((NZ + 2,)),
            dma((2 * NS,)), dma((2 * NS,)), dma((2 * NS,)), dma((2 * NS,)),
            dma((2, 4, NS)), dma((2, 4, NS)),
            dma((NP + 1,)), dma((NP + 1,)), dma((NP + 1,)), dma((NP + 1,)),
            dma, dma,
            dma((NS,)), dma((NS,)), dma((2, 2)), dma((2, 2)), dma((1 + NS,)),
        ],
        compiler_params=pltpu.CompilerParams(
            collective_id=0, has_side_effects=True, vmem_limit_bytes=60 * 2**20
        ),
        cost_estimate=pl.CostEstimate(
            flops=2 * 2 * 512 * FL * DL, bytes_accessed=20 * 2**20, transcendentals=2 * TOK * FL
        ),
    )(activations, pre_act, grad_act, quant_weight, block_scale)
    return pl.pallas_call(
        copy_out,
        out_shape=shapes,
        in_specs=[hbm] * 2,
        out_specs=(hbm, hbm),
        scratch_shapes=[pltpu.VMEM((TOK, DL), BF16), pltpu.VMEM((CH, FL), BF16), dma((2, 8))],
    )(*outs)


def solution(mesh):
    placed = (
        P(("row", "depth"), "col"),
        P(("col", "depth"), "row"),
        P(("col", "depth"), "row"),
        P("col", "row"),
        P("col", "row"),
    )
    return jax.shard_map(
        local,
        mesh=mesh,
        in_specs=placed,
        out_specs=(P(("row", "depth"), "col"), P(("col", "depth"), "row")),
        check_vma=False,
    )
```

```python
import jax
import jax.numpy as jnp
from jax import lax
from jax.experimental import pallas as pl
from jax.experimental.pallas import tpu as pltpu
from jax.sharding import PartitionSpec as P

MESH = pl.DeviceIdType.MESH
BF16, F32 = jnp.bfloat16, jnp.float32
NX, NY, NZ = 4, 4, 8
TOK = 128
FL = 2048
DL = 3712
CH = 232
FQ = 512
SLICES = ((0, 256), (256, 256), (512, 256), (768, 256), (1024, 512), (1536, 512))
NS = len(SLICES)
DIRECT = ()
WIN = 640
PAIR = 256
NP = 7
BASE = 1920
MID = 1792

inv_sqrt_two = 0.7071067811865476
inv_sqrt_tau = 0.3989422804014327


def gelu_slope(values):
    return (
        0.5 * (1.0 + lax.erf(values * inv_sqrt_two))
        + values * jnp.exp(-0.5 * values * values) * inv_sqrt_tau
    )


def kernel(
    acts_h, pre_h, grad_h, qw_h, scale_h, gi_h, gw_h,
    acts, pre, grad, scale, wq, wm, at32, asend, at, gb, zs, zr,
    gis, gism, gir, girm, gia, giam, gsx, go, gwo, own,
    in_sem, w_sem, a_send, a_recv, h_send, h_recv, g_send, g_recv, f_send, f_recv,
    z_send, z_recv, i_send, i_recv, j_send, j_recv, s_send, s_recv,
    n_send, n_recv, m_send, m_recv, out_sem,
):
    x, y, depth = lax.axis_index("row"), lax.axis_index("col"), lax.axis_index("depth")
    z, c = depth // 2, lax.rem(depth, 2)
    oc = 1 - c

    def dev(dx, dy, dz, core):
        return (
            lax.rem(x + dx, NX),
            lax.rem(y + dy, NY),
            lax.rem(z + dz, NZ) * 2 + core,
        )

    def remote(src, dst, send, recv, where):
        pltpu.make_async_remote_copy(
            src_ref=src, dst_ref=dst, send_sem=send, recv_sem=recv,
            device_id=where, device_id_type=MESH,
        ).start()

    def wait(ref, sem):
        pltpu.make_async_copy(ref, ref, sem).wait()

    head, tail = pl.ds(*SLICES[0]), pl.ds(SLICES[1][0], FL - SLICES[1][0])
    loads = [
        pltpu.make_async_copy(pre_h.at[:, head], pre.at[:, head], in_sem.at[0]),
        pltpu.make_async_copy(grad_h.at[:, head], grad.at[:, head], in_sem.at[1]),
        pltpu.make_async_copy(acts_h, acts, in_sem.at[2]),
        pltpu.make_async_copy(pre_h.at[:, tail], pre.at[:, tail], in_sem.at[3]),
        pltpu.make_async_copy(grad_h.at[:, tail], grad.at[:, tail], in_sem.at[4]),
        pltpu.make_async_copy(scale_h, scale, in_sem.at[5]),
    ]
    for cp in loads[:5]:
        cp.start()
    w_loads = [
        pltpu.make_async_copy(
            qw_h.at[pl.ds(pl.multiple_of(c * BASE + PAIR * i, 128), PAIR)], wq.at[i], w_sem.at[i]
        )
        for i in range(NP)
    ] + [pltpu.make_async_copy(qw_h.at[pl.ds(MID, 128)], wm, w_sem.at[NP])]

    partners = (
        [dev(dx, 0, 0, k) for dx in range(1, NX) for k in (c, oc)]
        + [dev(0, dy, 0, c) for dy in range(1, NY)]
        + [dev(0, 0, 1, c), dev(0, 0, NZ - 1, c), dev(0, 0, 0, oc)]
    )
    barrier = pltpu.get_barrier_semaphore()
    for who in partners:
        pl.semaphore_signal(barrier, inc=1, device_id=who, device_id_type=MESH)

    own_row = pl.multiple_of((c * NY + y) * TOK, TOK)

    def hidden(q):
        first, units = SLICES[q % NS]
        return pl.ds(first + q // NS * FL, units)

    def ship_slope(q):
        own = pl.ds(own_row, TOK)
        remote(
            gb.at[own, hidden(q)], gb.at[own, hidden(NS + q)], n_send.at[q], n_recv.at[q],
            dev(0, 0, NZ - 1 if q % 2 else 1, c),
        )

    def take_slope(q):
        wait(gb.at[pl.ds(0, TOK), hidden(q)], n_recv.at[q - NS])

    def slope(q):
        def rows(r, carry):
            at_r = pl.ds(pl.multiple_of(r * 16, 16), 16)
            cols = hidden(q)
            g = grad[at_r, cols].astype(F32) * gelu_slope(pre[at_r, cols].astype(F32))
            gb[pl.ds(pl.multiple_of(own_row + r * 16, 16), 16), cols] = g.astype(BF16)
            return carry

        lax.fori_loop(0, TOK // 16, rows, 0)

    def send_slope(q):
        block = gb.at[pl.ds(own_row, TOK), hidden(q)]
        for dy in (1, 3, 2):
            remote(block, block, g_send.at[q], g_recv.at[q], dev(0, dy, 0, c))

    def forward_slope(q):
        wait(gb.at[pl.ds(0, 3 * TOK), hidden(q)], g_recv.at[q])
        layer = gb.at[pl.ds(pl.multiple_of(c * NY * TOK, TOK), NY * TOK), hidden(q)]
        remote(layer, layer, f_send.at[q], f_recv.at[q], dev(0, 0, 0, oc))

    def wait_slope(q):
        wait(gb.at[pl.ds(0, NY * TOK), hidden(q)], f_recv.at[q])

    lanes = pl.ds(pl.multiple_of((c * NX + x) * TOK, TOK), TOK)

    def turn_acts(d):
        owner = lax.rem(z + d, NZ)
        tile = jnp.minimum(owner * (2 * CH) // 128, (DL - WIN) // 128)
        for i in range(WIN // 128):
            cols = pl.ds(pl.multiple_of((tile + i) * 128, 128), 128)
            at32[pl.ds(128 * i, 128), :] = acts[:, cols].astype(F32).T
        skip = owner * (2 * CH) - tile * 128
        for par in (0, 1):
            core = c if par == 0 else oc
            block = at32[pl.ds(pl.multiple_of(skip + core * CH, 8), CH), :].astype(BF16)
            asend[2 * d + par] = block
            if par == 0:
                at[d, :, lanes] = block

    def post_acts(d):
        for par in (0, 1):
            core = c if par == 0 else oc
            block = asend.at[2 * d + par]
            for dx in (1, 3, 2) if d in DIRECT else (1, 3):
                remote(block, at.at[d, :, lanes], a_send.at[d], a_recv.at[d], dev(dx, 0, 0, core))
            if par == 1:
                remote(block, at.at[d, :, lanes], a_send.at[d], a_recv.at[d], dev(0, 0, 0, oc))

    def send_acts(d):
        turn_acts(d)
        post_acts(d)

    def ship_acts():
        for way in (0, 1):
            for par in (0, 1):
                remote(
                    asend.at[8 + par], asend.at[2 * (NZ + way) + par], m_send.at[way, par],
                    m_recv.at[way, par], dev(0, 0, 1 if way == 0 else NZ - 1, c),
                )

    def take_acts(d):
        for par in (0, 1):
            wait(asend.at[2 * d + par], m_recv.at[d - NZ, par])
        at[d, :, lanes] = asend[2 * d]
        post_acts(d)

    def hand_on(d):
        wait(at.at[d, :, pl.ds(0, 5 * TOK)], a_recv.at[d])
        for dx, core in ((1, c), (3, oc)):
            block = at.at[
                d, :, pl.ds(pl.multiple_of((core * NX + lax.rem(x - dx + NX, NX)) * TOK, TOK), TOK)
            ]
            remote(block, block, h_send.at[d], h_recv.at[d], dev(dx, 0, 0, c))

    def wait_acts(d):
        if d in DIRECT:
            wait(at.at[d, :, pl.ds(0, 7 * TOK)], a_recv.at[d])
        else:
            wait(at.at[d, :, pl.ds(0, 2 * TOK)], h_recv.at[d])

    def part(d, q):
        return lax.dot_general(
            at[d], gb[:, hidden(q)], (((1,), (0,)), ((), ())),
            preferred_element_type=F32,
        )

    def is_long(way, q):
        return q % 2 == way

    def landing(way, r, q):
        return zr.at[way, r, :, hidden(q)]

    def ring(way, r, q):
        long = is_long(way, q)
        offset = (4 if long else 3) - r
        mine = part(offset if way == 0 else NZ - offset, q)
        if r == 0 or (long and r == 1):
            src = zs.at[way, :, hidden(q)]
            if long:
                mine = mine + part(NZ + way, NS + q)
        else:
            src = landing(way, r - 1, q)
            wait(src, z_recv.at[way, r - 1, q])
            mine = mine + src[...].astype(F32)
        src[...] = mine.astype(BF16)
        remote(
            src, landing(way, r, q), z_send.at[way, r, q], z_recv.at[way, r, q],
            dev(0, 0, 1 if way == 0 else NZ - 1, c),
        )

    def add_short(q):
        way = 1 if is_long(0, q) else 0
        total = part(0, q)
        wait(landing(way, 2, q), z_recv.at[way, 2, q])
        own[:, hidden(q)] = total + landing(way, 2, q)[...].astype(F32)

    def add_long(q):
        way = 0 if is_long(0, q) else 1
        wait(landing(way, 3, q), z_recv.at[way, 3, q])
        gwo[:, hidden(q)] = (own[:, hidden(q)] + landing(way, 3, q)[...].astype(F32)).astype(BF16)
        pltpu.make_async_copy(
            gwo.at[:, hidden(q)], gw_h.at[:, hidden(q)], out_sem.at[1 + q]
        ).start()

    nt = (((1,), (1,)), ((), ()))

    def rescale(ref, row):
        by = scale[pl.ds(row, 1), :]

        def rows(r, carry):
            at_r = pl.ds(pl.multiple_of(r * 16, 16), 16)
            ref[at_r, :] = (ref[at_r, :].astype(F32) * by).astype(BF16)
            return carry

        lax.fori_loop(0, 8, rows, 0)

    def inputs(i):
        w_loads[i].wait()
        if i < NP:
            for h in (0, 1):
                rescale(wq.at[i, pl.ds(128 * h, 128)], c * 15 + 2 * i + h)
            for k in (0, 1):
                got = lax.dot_general(
                    gb[pl.ds(k * NX * TOK, NX * TOK), pl.ds(0, FL)], wq[i], nt, preferred_element_type=F32
                )
                gis[i, k] = got.reshape(NX, TOK, PAIR).astype(BF16)
            far = lax.rem(x + 2, NX)
            for k, dx in ((0, 1), (1, 3)):
                remote(
                    gis.at[i, k, far], gia.at[i, k], j_send.at[i], j_recv.at[i], dev(dx, 0, 0, c)
                )
        else:
            rescale(wm, 14)
            got = lax.dot_general(
                gb[pl.ds(pl.multiple_of(c * NX * TOK, TOK), NX * TOK), pl.ds(0, FL)], wm[...], nt,
                preferred_element_type=F32,
            )
            gism[...] = got.reshape(NX, TOK, 128).astype(BF16)
            far = lax.rem(x + 2, NX)
            for k, dx in ((0, 1), (1, 3)):
                remote(
                    gism.at[far, pl.ds(64 * k, 64)], giam.at[k], j_send.at[i], j_recv.at[i],
                    dev(dx, 0, 0, c),
                )

    def inputs_on(i):
        wait(gia.at[i] if i < NP else giam, j_recv.at[i])
        for k, dx in ((0, 1), (1, 3)):
            to = lax.rem(x + dx, NX)
            if i < NP:
                mine, came = gis.at[i, k, to], gia.at[i, k]
            else:
                mine, came = gism.at[to, pl.ds(64 * k, 64)], giam.at[k]
            mine[...] = (mine[...].astype(F32) + came[...].astype(F32)).astype(BF16)
            if i < NP:
                remote(gis.at[i, :, to], gir.at[i, k], i_send.at[i], i_recv.at[i], dev(dx, 0, 0, c))
            else:
                remote(gism.at[to], girm.at[k], i_send.at[i], i_recv.at[i], dev(dx, 0, 0, c))

    def inputs_done(i):
        if i < NP:
            wait(gir.at[i], i_recv.at[i])
            cols = pl.ds(pl.multiple_of(c * BASE + PAIR * i, 128), PAIR)

            def total(k):
                got = gis[i, pl.ds(k, 1), pl.ds(x, 1)].reshape(TOK, PAIR).astype(F32)
                for s in range(2):
                    got = got + gir[i, s, pl.ds(k, 1)].reshape(TOK, PAIR).astype(F32)
                return got.astype(BF16)

            gsx[i] = total(oc)
            remote(gsx.at[i], go.at[:, cols], s_send, s_recv, dev(0, 0, 0, oc))
            go[:, cols] = total(c)
        else:
            wait(girm, i_recv.at[i])
            got = gism[pl.ds(x, 1)].reshape(TOK, 128).astype(F32)
            for s in range(2):
                got = got + girm[s].astype(F32)
            go[:, pl.ds(MID, 128)] = got.astype(BF16)

    handed, here, summed, scaled = set(), set(), set(), False

    def get(d):
        if d not in here:
            if d not in DIRECT:
                pass_on(d)
            wait_acts(d)
            here.add(d)

    def step(way, r, q):
        offset = (4 if is_long(way, q) else 3) - r
        get(offset if way == 0 else NZ - offset)
        if r == 1 and is_long(way, q):
            get(NZ + way)
        ring(way, r, q)

    def pass_on(d):
        if d not in handed:
            hand_on(d)
            handed.add(d)

    def spread(q):
        take_slope(q)
        send_slope(q)

    def own_slice(q):
        slope(q)
        ship_slope(q)

    loads[0].wait()
    loads[1].wait()
    slope(0)
    pl.semaphore_wait(barrier, len(partners))
    send_slope(0)
    loads[2].wait()
    turn_acts(4)
    ship_acts()
    ship_slope(0)
    send_acts(5)
    send_acts(3)
    loads[3].wait()
    loads[4].wait()
    own_slice(1)
    send_slope(1)

    def load_weight(_):
        for cp in [loads[5]] + w_loads:
            cp.start()

    plan = (
        ("S2 S5 F0 G2", "S4 H5 W0 A2", "S3 H3 F1 G3", "G4 G5 U6 A6", "F2 100 W1 H2",)
        + ("L0 001 A1 W2", "102 F3 H6 U7", "U8 U9 W3 003", "A7 U10 011 H1", "F4 U11 112 110",)
        + ("T8 013 H7 W4", "104 T9 021 F5", "A0 H8 023 122", "120 F6 W5 005", "I6 W6 F7 H9",)
        + ("I3 W7 010 114", "F8 H0 I1 F9", "W8 015 I5 W9", "113 012 F10 111", "J1 124 J5 W10",)
        + ("014 025 J3 F11", "I0 022 W11 115", "121 D5 D1 J6", "020 D3 024 J0", "I7 123 I2 D6",)
        + ("125 I4 032 D0", "J2 131 J7 030", "133 J4 D2 D7", "034 135 D4",)
    )
    does = dict(
        F=forward_slope, A=send_acts, W=wait_slope, H=pass_on, S=own_slice,
        G=send_slope, L=load_weight, T=take_acts, U=spread, I=inputs, J=inputs_on, D=inputs_done,
    )
    for word in " ".join(plan).split():
        if word[0] == "I" and not scaled:
            loads[5].wait()
            scaled = True
        if word[0] == "D":
            summed.add(int(word[1:]))
        if word[0] in does:
            does[word[0]](int(word[1:]))
        else:
            step(*map(int, word))
    if 0 not in here:
        wait_acts(0)
    for q in range(NS):
        add_short(q)
    for i in range(NP + 1):
        if i not in summed:
            inputs_done(i)
    wait(go.at[:, pl.ds(0, MID)], s_recv)
    out_i = pltpu.make_async_copy(go, gi_h, out_sem.at[0])
    out_i.start()
    for q in range(NS):
        add_long(q)

    for q in range(NS):
        wait(gb.at[pl.ds(0, 3 * TOK), hidden(q)], g_send.at[q])
        wait(gb.at[pl.ds(0, NY * TOK), hidden(q)], f_send.at[q])
    for q in range(NS, 2 * NS):
        wait(gb.at[pl.ds(0, 3 * TOK), hidden(q)], g_send.at[q])
        wait(gb.at[pl.ds(0, NY * TOK), hidden(q)], f_send.at[q])
        wait(gb.at[pl.ds(0, TOK), hidden(q)], n_send.at[q - NS])
    for way in (0, 1):
        for par in (0, 1):
            wait(asend.at[8 + par], m_send.at[way, par])
    for d in (0, 1, 2, 3, 5, 6, 7, 8, 9):
        wait(at.at[d, :, pl.ds(0, (7 if d in DIRECT else 5) * TOK)], a_send.at[d])
        if d not in DIRECT:
            wait(at.at[d, :, pl.ds(0, 2 * TOK)], h_send.at[d])
    for way in (0, 1):
        for q in range(NS):
            for r in range(1, 4) if is_long(way, q) else range(3):
                wait(landing(way, r, q), z_send.at[way, r, q])
    for i in range(NP):
        wait(gia.at[i], j_send.at[i])
        wait(gir.at[i], i_send.at[i])
    wait(giam, j_send.at[NP])
    wait(girm, i_send.at[NP])
    wait(go.at[:, pl.ds(0, MID)], s_send)
    out_i.wait()
    for q in range(NS):
        wait(gwo.at[:, hidden(q)], out_sem.at[1 + q])


def copy_out(gi_in, gw_in, gi_out, gw_out, gi, gw, sem):
    pieces = [(pl.ds(32 * i, 32), slice(None)) for i in range(4)]
    bands = [(slice(None), pl.ds(FQ * i, FQ)) for i in range(4)]
    steps = [(gi_in.at[k], gi.at[k], gi_out.at[k]) for k in pieces] + [
        (gw_in.at[k], gw.at[k], gw_out.at[k]) for k in bands
    ]
    into = [pltpu.make_async_copy(src, mid, sem.at[0, i]) for i, (src, mid, _) in enumerate(steps)]
    out = [pltpu.make_async_copy(mid, dst, sem.at[1, i]) for i, (_, mid, dst) in enumerate(steps)]
    for cp in into:
        cp.start()
    for one, two in zip(into, out):
        one.wait()
        two.start()
    for cp in out:
        cp.wait()


def local(activations, pre_act, grad_act, quant_weight, block_scale):
    dma = pltpu.SemaphoreType.DMA
    hbm = pl.BlockSpec(memory_space=pl.ANY)
    shapes = (
        jax.ShapeDtypeStruct((TOK, DL), BF16),
        jax.ShapeDtypeStruct((CH, FL), BF16),
    )
    outs = pl.pallas_call(
        kernel,
        out_shape=shapes,
        in_specs=[hbm] * 5,
        out_specs=(hbm, hbm),
        scratch_shapes=[
            pltpu.VMEM((TOK, DL), BF16),
            pltpu.VMEM((TOK, FL), BF16),
            pltpu.VMEM((TOK, FL), BF16),
            pltpu.VMEM((29, FL), F32),
            pltpu.VMEM((NP, PAIR, FL), BF16),
            pltpu.VMEM((128, FL), BF16),
            pltpu.VMEM((WIN, TOK), F32),
            pltpu.VMEM((2 * NZ + 4, CH, TOK), BF16),
            pltpu.VMEM((NZ + 2, CH, 8 * TOK), BF16),
            pltpu.VMEM((8 * TOK, 2 * FL), BF16),
            pltpu.VMEM((2, CH, FL), BF16),
            pltpu.VMEM((2, 4, CH, FL), BF16),
            pltpu.VMEM((NP, 2, NX, TOK, PAIR), BF16),
            pltpu.VMEM((NX, TOK, 128), BF16),
            pltpu.VMEM((NP, 2, 2, TOK, PAIR), BF16),
            pltpu.VMEM((2, TOK, 128), BF16),
            pltpu.VMEM((NP, 2, TOK, PAIR), BF16),
            pltpu.VMEM((2, 64, 128), BF16),
            pltpu.VMEM((NP, TOK, PAIR), BF16),
            pltpu.VMEM((TOK, DL), BF16),
            pltpu.VMEM((CH, FL), BF16),
            pltpu.VMEM((CH, FL), F32),
            dma((6,)), dma((NP + 1,)),
            dma((NZ + 2,)), dma((NZ + 2,)), dma((NZ + 2,)), dma((NZ + 2,)),
            dma((2 * NS,)), dma((2 * NS,)), dma((2 * NS,)), dma((2 * NS,)),
            dma((2, 4, NS)), dma((2, 4, NS)),
            dma((NP + 1,)), dma((NP + 1,)), dma((NP + 1,)), dma((NP + 1,)),
            dma, dma,
            dma((NS,)), dma((NS,)), dma((2, 2)), dma((2, 2)), dma((1 + NS,)),
        ],
        compiler_params=pltpu.CompilerParams(
            collective_id=0, has_side_effects=True, vmem_limit_bytes=60 * 2**20
        ),
        cost_estimate=pl.CostEstimate(
            flops=2 * 2 * 512 * FL * DL, bytes_accessed=20 * 2**20, transcendentals=2 * TOK * FL
        ),
    )(activations, pre_act, grad_act, quant_weight, block_scale)
    return pl.pallas_call(
        copy_out,
        out_shape=shapes,
        in_specs=[hbm] * 2,
        out_specs=(hbm, hbm),
        scratch_shapes=[pltpu.VMEM((TOK, DL), BF16), pltpu.VMEM((CH, FL), BF16), dma((2, 8))],
    )(*outs)


def solution(mesh):
    placed = (
        P(("row", "depth"), "col"),
        P(("col", "depth"), "row"),
        P(("col", "depth"), "row"),
        P("col", "row"),
        P("col", "row"),
    )
    return jax.shard_map(
        local,
        mesh=mesh,
        in_specs=placed,
        out_specs=(P(("row", "depth"), "col"), P(("col", "depth"), "row")),
        check_vma=False,
    )
```

```python
import jax
import jax.numpy as jnp
from jax import lax
from jax.experimental import pallas as pl
from jax.experimental.pallas import tpu as pltpu
from jax.sharding import PartitionSpec as P

MESH = pl.DeviceIdType.MESH
BF16, F32 = jnp.bfloat16, jnp.float32
NX, NY, NZ = 4, 4, 8
TOK = 128
FL = 2048
DL = 3712
CH = 232
FQ = 512
SLICES = ((0, 256), (256, 256), (512, 256), (768, 256), (1024, 512), (1536, 512))
NS = len(SLICES)
DIRECT = ()
WIN = 640
PAIR = 256
NP = 7
BASE = 1920
MID = 1792

inv_sqrt_two = 0.7071067811865476
inv_sqrt_tau = 0.3989422804014327


def gelu_slope(values):
    return (
        0.5 * (1.0 + lax.erf(values * inv_sqrt_two))
        + values * jnp.exp(-0.5 * values * values) * inv_sqrt_tau
    )


def kernel(
    acts_h, pre_h, grad_h, qw_h, scale_h, gi_h, gw_h,
    acts, pre, grad, scale, wq, wm, at32, asend, at, gb, zs, zr,
    gis, gism, gir, girm, gia, giam, gsx, go, gwo, own,
    in_sem, w_sem, a_send, a_recv, h_send, h_recv, g_send, g_recv, f_send, f_recv,
    z_send, z_recv, i_send, i_recv, j_send, j_recv, s_send, s_recv,
    n_send, n_recv, m_send, m_recv, out_sem,
):
    x, y, depth = lax.axis_index("row"), lax.axis_index("col"), lax.axis_index("depth")
    z, c = depth // 2, lax.rem(depth, 2)
    oc = 1 - c

    def dev(dx, dy, dz, core):
        return (
            lax.rem(x + dx, NX),
            lax.rem(y + dy, NY),
            lax.rem(z + dz, NZ) * 2 + core,
        )

    def remote(src, dst, send, recv, where):
        pltpu.make_async_remote_copy(
            src_ref=src, dst_ref=dst, send_sem=send, recv_sem=recv,
            device_id=where, device_id_type=MESH,
        ).start()

    def wait(ref, sem):
        pltpu.make_async_copy(ref, ref, sem).wait()

    head, tail = pl.ds(*SLICES[0]), pl.ds(SLICES[1][0], FL - SLICES[1][0])
    loads = [
        pltpu.make_async_copy(pre_h.at[:, head], pre.at[:, head], in_sem.at[0]),
        pltpu.make_async_copy(grad_h.at[:, head], grad.at[:, head], in_sem.at[1]),
        pltpu.make_async_copy(acts_h, acts, in_sem.at[2]),
        pltpu.make_async_copy(pre_h.at[:, tail], pre.at[:, tail], in_sem.at[3]),
        pltpu.make_async_copy(grad_h.at[:, tail], grad.at[:, tail], in_sem.at[4]),
        pltpu.make_async_copy(scale_h, scale, in_sem.at[5]),
    ]
    for cp in loads[:5]:
        cp.start()
    w_loads = [
        pltpu.make_async_copy(
            qw_h.at[pl.ds(pl.multiple_of(c * BASE + PAIR * i, 128), PAIR)], wq.at[i], w_sem.at[i]
        )
        for i in range(NP)
    ] + [pltpu.make_async_copy(qw_h.at[pl.ds(MID, 128)], wm, w_sem.at[NP])]

    partners = (
        [dev(dx, 0, 0, k) for dx in range(1, NX) for k in (c, oc)]
        + [dev(0, dy, 0, c) for dy in range(1, NY)]
        + [dev(0, 0, 1, c), dev(0, 0, NZ - 1, c), dev(0, 0, 0, oc)]
    )
    barrier = pltpu.get_barrier_semaphore()
    for who in partners:
        pl.semaphore_signal(barrier, inc=1, device_id=who, device_id_type=MESH)

    own_row = pl.multiple_of((c * NY + y) * TOK, TOK)

    def hidden(q):
        first, units = SLICES[q % NS]
        return pl.ds(first + q // NS * FL, units)

    def ship_slope(q):
        own = pl.ds(own_row, TOK)
        remote(
            gb.at[own, hidden(q)], gb.at[own, hidden(NS + q)], n_send.at[q], n_recv.at[q],
            dev(0, 0, NZ - 1 if q % 2 else 1, c),
        )

    def take_slope(q):
        wait(gb.at[pl.ds(0, TOK), hidden(q)], n_recv.at[q - NS])

    def slope(q):
        def rows(r, carry):
            at_r = pl.ds(pl.multiple_of(r * 16, 16), 16)
            cols = hidden(q)
            g = grad[at_r, cols].astype(F32) * gelu_slope(pre[at_r, cols].astype(F32))
            gb[pl.ds(pl.multiple_of(own_row + r * 16, 16), 16), cols] = g.astype(BF16)
            return carry

        lax.fori_loop(0, TOK // 16, rows, 0)

    def send_slope(q):
        block = gb.at[pl.ds(own_row, TOK), hidden(q)]
        for dy in (1, 3, 2):
            remote(block, block, g_send.at[q], g_recv.at[q], dev(0, dy, 0, c))

    def forward_slope(q):
        wait(gb.at[pl.ds(0, 3 * TOK), hidden(q)], g_recv.at[q])
        layer = gb.at[pl.ds(pl.multiple_of(c * NY * TOK, TOK), NY * TOK), hidden(q)]
        remote(layer, layer, f_send.at[q], f_recv.at[q], dev(0, 0, 0, oc))

    def wait_slope(q):
        wait(gb.at[pl.ds(0, NY * TOK), hidden(q)], f_recv.at[q])

    lanes = pl.ds(pl.multiple_of((c * NX + x) * TOK, TOK), TOK)

    def turn_acts(d):
        owner = lax.rem(z + d, NZ)
        tile = jnp.minimum(owner * (2 * CH) // 128, (DL - WIN) // 128)
        for i in range(WIN // 128):
            cols = pl.ds(pl.multiple_of((tile + i) * 128, 128), 128)
            at32[pl.ds(128 * i, 128), :] = acts[:, cols].astype(F32).T
        skip = owner * (2 * CH) - tile * 128
        for par in (0, 1):
            core = c if par == 0 else oc
            block = at32[pl.ds(pl.multiple_of(skip + core * CH, 8), CH), :].astype(BF16)
            asend[2 * d + par] = block
            if par == 0:
                at[d, :, lanes] = block

    def post_acts(d):
        for par in (0, 1):
            core = c if par == 0 else oc
            block = asend.at[2 * d + par]
            for dx in (1, 3, 2) if d in DIRECT else (1, 3):
                remote(block, at.at[d, :, lanes], a_send.at[d], a_recv.at[d], dev(dx, 0, 0, core))
            if par == 1:
                remote(block, at.at[d, :, lanes], a_send.at[d], a_recv.at[d], dev(0, 0, 0, oc))

    def send_acts(d):
        turn_acts(d)
        post_acts(d)

    def ship_acts():
        for way in (0, 1):
            for par in (0, 1):
                remote(
                    asend.at[8 + par], asend.at[2 * (NZ + way) + par], m_send.at[way, par],
                    m_recv.at[way, par], dev(0, 0, 1 if way == 0 else NZ - 1, c),
                )

    def take_acts(d):
        for par in (0, 1):
            wait(asend.at[2 * d + par], m_recv.at[d - NZ, par])
        at[d, :, lanes] = asend[2 * d]
        post_acts(d)

    def hand_on(d):
        wait(at.at[d, :, pl.ds(0, 5 * TOK)], a_recv.at[d])
        for dx, core in ((1, c), (3, oc)):
            block = at.at[
                d, :, pl.ds(pl.multiple_of((core * NX + lax.rem(x - dx + NX, NX)) * TOK, TOK), TOK)
            ]
            remote(block, block, h_send.at[d], h_recv.at[d], dev(dx, 0, 0, c))

    def wait_acts(d):
        if d in DIRECT:
            wait(at.at[d, :, pl.ds(0, 7 * TOK)], a_recv.at[d])
        else:
            wait(at.at[d, :, pl.ds(0, 2 * TOK)], h_recv.at[d])

    def part(d, q):
        return lax.dot_general(
            at[d], gb[:, hidden(q)], (((1,), (0,)), ((), ())),
            preferred_element_type=F32,
        )

    def is_long(way, q):
        return q % 2 == way

    def landing(way, r, q):
        return zr.at[way, r, :, hidden(q)]

    def ring(way, r, q):
        long = is_long(way, q)
        offset = (4 if long else 3) - r
        mine = part(offset if way == 0 else NZ - offset, q)
        if r == 0 or (long and r == 1):
            src = zs.at[way, :, hidden(q)]
            if long:
                mine = mine + part(NZ + way, NS + q)
        else:
            src = landing(way, r - 1, q)
            wait(src, z_recv.at[way, r - 1, q])
            mine = mine + src[...].astype(F32)
        src[...] = mine.astype(BF16)
        remote(
            src, landing(way, r, q), z_send.at[way, r, q], z_recv.at[way, r, q],
            dev(0, 0, 1 if way == 0 else NZ - 1, c),
        )

    def add_short(q):
        way = 1 if is_long(0, q) else 0
        total = part(0, q)
        wait(landing(way, 2, q), z_recv.at[way, 2, q])
        own[:, hidden(q)] = total + landing(way, 2, q)[...].astype(F32)

    def add_long(q):
        way = 0 if is_long(0, q) else 1
        wait(landing(way, 3, q), z_recv.at[way, 3, q])
        gwo[:, hidden(q)] = (own[:, hidden(q)] + landing(way, 3, q)[...].astype(F32)).astype(BF16)
        pltpu.make_async_copy(
            gwo.at[:, hidden(q)], gw_h.at[:, hidden(q)], out_sem.at[1 + q]
        ).start()

    nt = (((1,), (1,)), ((), ()))

    def rescale(ref, row):
        by = scale[pl.ds(row, 1), :]

        def rows(r, carry):
            at_r = pl.ds(pl.multiple_of(r * 16, 16), 16)
            ref[at_r, :] = (ref[at_r, :].astype(F32) * by).astype(BF16)
            return carry

        lax.fori_loop(0, 8, rows, 0)

    def inputs(i):
        w_loads[i].wait()
        if i < NP:
            for h in (0, 1):
                rescale(wq.at[i, pl.ds(128 * h, 128)], c * 15 + 2 * i + h)
            for k in (0, 1):
                got = lax.dot_general(
                    gb[pl.ds(k * NX * TOK, NX * TOK), pl.ds(0, FL)], wq[i], nt, preferred_element_type=F32
                )
                gis[i, k] = got.reshape(NX, TOK, PAIR).astype(BF16)
            far = lax.rem(x + 2, NX)
            for k, dx in ((0, 1), (1, 3)):
                remote(
                    gis.at[i, k, far], gia.at[i, k], j_send.at[i], j_recv.at[i], dev(dx, 0, 0, c)
                )
        else:
            rescale(wm, 14)
            got = lax.dot_general(
                gb[pl.ds(pl.multiple_of(c * NX * TOK, TOK), NX * TOK), pl.ds(0, FL)], wm[...], nt,
                preferred_element_type=F32,
            )
            gism[...] = got.reshape(NX, TOK, 128).astype(BF16)
            far = lax.rem(x + 2, NX)
            for k, dx in ((0, 1), (1, 3)):
                remote(
                    gism.at[far, pl.ds(64 * k, 64)], giam.at[k], j_send.at[i], j_recv.at[i],
                    dev(dx, 0, 0, c),
                )

    def inputs_on(i):
        wait(gia.at[i] if i < NP else giam, j_recv.at[i])
        for k, dx in ((0, 1), (1, 3)):
            to = lax.rem(x + dx, NX)
            if i < NP:
                mine, came = gis.at[i, k, to], gia.at[i, k]
            else:
                mine, came = gism.at[to, pl.ds(64 * k, 64)], giam.at[k]
            mine[...] = (mine[...].astype(F32) + came[...].astype(F32)).astype(BF16)
            if i < NP:
                remote(gis.at[i, :, to], gir.at[i, k], i_send.at[i], i_recv.at[i], dev(dx, 0, 0, c))
            else:
                remote(gism.at[to], girm.at[k], i_send.at[i], i_recv.at[i], dev(dx, 0, 0, c))

    def inputs_done(i):
        if i < NP:
            wait(gir.at[i], i_recv.at[i])
            cols = pl.ds(pl.multiple_of(c * BASE + PAIR * i, 128), PAIR)

            def total(k):
                got = gis[i, pl.ds(k, 1), pl.ds(x, 1)].reshape(TOK, PAIR).astype(F32)
                for s in range(2):
                    got = got + gir[i, s, pl.ds(k, 1)].reshape(TOK, PAIR).astype(F32)
                return got.astype(BF16)

            gsx[i] = total(oc)
            remote(gsx.at[i], go.at[:, cols], s_send, s_recv, dev(0, 0, 0, oc))
            go[:, cols] = total(c)
        else:
            wait(girm, i_recv.at[i])
            got = gism[pl.ds(x, 1)].reshape(TOK, 128).astype(F32)
            for s in range(2):
                got = got + girm[s].astype(F32)
            go[:, pl.ds(MID, 128)] = got.astype(BF16)

    handed, here, summed, scaled = set(), set(), set(), False

    def get(d):
        if d not in here:
            if d not in DIRECT:
                pass_on(d)
            wait_acts(d)
            here.add(d)

    def step(way, r, q):
        offset = (4 if is_long(way, q) else 3) - r
        get(offset if way == 0 else NZ - offset)
        if r == 1 and is_long(way, q):
            get(NZ + way)
        ring(way, r, q)

    def pass_on(d):
        if d not in handed:
            hand_on(d)
            handed.add(d)

    def spread(q):
        take_slope(q)
        send_slope(q)

    def own_slice(q):
        slope(q)
        ship_slope(q)

    loads[0].wait()
    loads[1].wait()
    slope(0)
    pl.semaphore_wait(barrier, len(partners))
    send_slope(0)
    loads[2].wait()
    turn_acts(4)
    ship_acts()
    ship_slope(0)
    send_acts(5)
    send_acts(3)
    loads[3].wait()
    loads[4].wait()
    own_slice(1)
    send_slope(1)

    def load_weight(_):
        for cp in [loads[5]] + w_loads:
            cp.start()

    plan = (
        ("S2 S5 F0 G2", "S4 H5 W0 A2", "S3 H3 F1 G3", "G4 G5 U6 A6", "F2 100 W1 H2",)
        + ("L0 001 A1 W2", "102 F3 H6 U7", "U8 U9 W3 003", "A7 U10 011 H1", "F4 U11 112 110",)
        + ("T8 013 H7 W4", "104 T9 021 F5", "A0 H8 023 122", "120 F6 W5 005", "I6 W6 F7 H9",)
        + ("I3 W7 010 114", "F8 H0 I1 F9", "W8 015 I5 W9", "113 012 F10 111", "J1 124 J5 W10",)
        + ("014 025 J3 F11", "I0 022 W11 115", "121 D5 D1 J6", "020 D3 024 J0", "I7 123 I2 D6",)
        + ("125 I4 032 D0", "J2 131 J7 030", "133 J4 D2 D7", "034 135 D4",)
    )
    does = dict(
        F=forward_slope, A=send_acts, W=wait_slope, H=pass_on, S=own_slice,
        G=send_slope, L=load_weight, T=take_acts, U=spread, I=inputs, J=inputs_on, D=inputs_done,
    )
    for word in " ".join(plan).split():
        if word[0] == "I" and not scaled:
            loads[5].wait()
            scaled = True
        if word[0] == "D":
            summed.add(int(word[1:]))
        if word[0] in does:
            does[word[0]](int(word[1:]))
        else:
            step(*map(int, word))
    if 0 not in here:
        wait_acts(0)
    for q in range(NS):
        add_short(q)
    for i in range(NP + 1):
        if i not in summed:
            inputs_done(i)
    for q in range(NS):
        wait(gb.at[pl.ds(0, 3 * TOK), hidden(q)], g_send.at[q])
        wait(gb.at[pl.ds(0, NY * TOK), hidden(q)], f_send.at[q])
    for q in range(NS, 2 * NS):
        wait(gb.at[pl.ds(0, 3 * TOK), hidden(q)], g_send.at[q])
        wait(gb.at[pl.ds(0, NY * TOK), hidden(q)], f_send.at[q])
        wait(gb.at[pl.ds(0, TOK), hidden(q)], n_send.at[q - NS])
    for way in (0, 1):
        for par in (0, 1):
            wait(asend.at[8 + par], m_send.at[way, par])
    for d in (0, 1, 2, 3, 5, 6, 7, 8, 9):
        wait(at.at[d, :, pl.ds(0, (7 if d in DIRECT else 5) * TOK)], a_send.at[d])
        if d not in DIRECT:
            wait(at.at[d, :, pl.ds(0, 2 * TOK)], h_send.at[d])
    for way in (0, 1):
        for q in range(NS):
            for r in range(1, 3) if is_long(way, q) else range(3):
                wait(landing(way, r, q), z_send.at[way, r, q])
    for i in range(NP):
        wait(gia.at[i], j_send.at[i])
        wait(gir.at[i], i_send.at[i])
    wait(giam, j_send.at[NP])
    wait(girm, i_send.at[NP])
    wait(go.at[:, pl.ds(0, MID)], s_recv)
    out_i = pltpu.make_async_copy(go, gi_h, out_sem.at[0])
    out_i.start()
    for q in range(NS):
        add_long(q)

    for q in range(NS):
        way = 0 if is_long(0, q) else 1
        wait(landing(way, 3, q), z_send.at[way, 3, q])
    wait(go.at[:, pl.ds(0, MID)], s_send)
    out_i.wait()
    for q in range(NS):
        wait(gwo.at[:, hidden(q)], out_sem.at[1 + q])


def copy_out(gi_in, gw_in, gi_out, gw_out, gi, gw, sem):
    pieces = [(pl.ds(32 * i, 32), slice(None)) for i in range(4)]
    bands = [(slice(None), pl.ds(FQ * i, FQ)) for i in range(4)]
    steps = [(gi_in.at[k], gi.at[k], gi_out.at[k]) for k in pieces] + [
        (gw_in.at[k], gw.at[k], gw_out.at[k]) for k in bands
    ]
    into = [pltpu.make_async_copy(src, mid, sem.at[0, i]) for i, (src, mid, _) in enumerate(steps)]
    out = [pltpu.make_async_copy(mid, dst, sem.at[1, i]) for i, (_, mid, dst) in enumerate(steps)]
    for cp in into:
        cp.start()
    for one, two in zip(into, out):
        one.wait()
        two.start()
    for cp in out:
        cp.wait()


def local(activations, pre_act, grad_act, quant_weight, block_scale):
    dma = pltpu.SemaphoreType.DMA
    hbm = pl.BlockSpec(memory_space=pl.ANY)
    shapes = (
        jax.ShapeDtypeStruct((TOK, DL), BF16),
        jax.ShapeDtypeStruct((CH, FL), BF16),
    )
    outs = pl.pallas_call(
        kernel,
        out_shape=shapes,
        in_specs=[hbm] * 5,
        out_specs=(hbm, hbm),
        scratch_shapes=[
            pltpu.VMEM((TOK, DL), BF16),
            pltpu.VMEM((TOK, FL), BF16),
            pltpu.VMEM((TOK, FL), BF16),
            pltpu.VMEM((29, FL), F32),
            pltpu.VMEM((NP, PAIR, FL), BF16),
            pltpu.VMEM((128, FL), BF16),
            pltpu.VMEM((WIN, TOK), F32),
            pltpu.VMEM((2 * NZ + 4, CH, TOK), BF16),
            pltpu.VMEM((NZ + 2, CH, 8 * TOK), BF16),
            pltpu.VMEM((8 * TOK, 2 * FL), BF16),
            pltpu.VMEM((2, CH, FL), BF16),
            pltpu.VMEM((2, 4, CH, FL), BF16),
            pltpu.VMEM((NP, 2, NX, TOK, PAIR), BF16),
            pltpu.VMEM((NX, TOK, 128), BF16),
            pltpu.VMEM((NP, 2, 2, TOK, PAIR), BF16),
            pltpu.VMEM((2, TOK, 128), BF16),
            pltpu.VMEM((NP, 2, TOK, PAIR), BF16),
            pltpu.VMEM((2, 64, 128), BF16),
            pltpu.VMEM((NP, TOK, PAIR), BF16),
            pltpu.VMEM((TOK, DL), BF16),
            pltpu.VMEM((CH, FL), BF16),
            pltpu.VMEM((CH, FL), F32),
            dma((6,)), dma((NP + 1,)),
            dma((NZ + 2,)), dma((NZ + 2,)), dma((NZ + 2,)), dma((NZ + 2,)),
            dma((2 * NS,)), dma((2 * NS,)), dma((2 * NS,)), dma((2 * NS,)),
            dma((2, 4, NS)), dma((2, 4, NS)),
            dma((NP + 1,)), dma((NP + 1,)), dma((NP + 1,)), dma((NP + 1,)),
            dma, dma,
            dma((NS,)), dma((NS,)), dma((2, 2)), dma((2, 2)), dma((1 + NS,)),
        ],
        compiler_params=pltpu.CompilerParams(
            collective_id=0, has_side_effects=True, vmem_limit_bytes=60 * 2**20
        ),
        cost_estimate=pl.CostEstimate(
            flops=2 * 2 * 512 * FL * DL, bytes_accessed=20 * 2**20, transcendentals=2 * TOK * FL
        ),
    )(activations, pre_act, grad_act, quant_weight, block_scale)
    return pl.pallas_call(
        copy_out,
        out_shape=shapes,
        in_specs=[hbm] * 2,
        out_specs=(hbm, hbm),
        scratch_shapes=[pltpu.VMEM((TOK, DL), BF16), pltpu.VMEM((CH, FL), BF16), dma((2, 8))],
    )(*outs)


def solution(mesh):
    placed = (
        P(("row", "depth"), "col"),
        P(("col", "depth"), "row"),
        P(("col", "depth"), "row"),
        P("col", "row"),
        P("col", "row"),
    )
    return jax.shard_map(
        local,
        mesh=mesh,
        in_specs=placed,
        out_specs=(P(("row", "depth"), "col"), P(("col", "depth"), "row")),
        check_vma=False,
    )
```
